512 devices in a mesh: wide: 128 (over y, z, x_lo), mp: 4 (over x_hi, core).
Axes of the slice: x: 4 (x_hi: 2, x_lo: 2; x = x_hi * 2 + x_lo), y: 4, z: 16, core: 2. Of those that a mesh axis runs over, the one named last changes fastest.
Arguments:
- clip_feats: bfloat16 [16384, 768], P('wide'), may hold values from -6 to 6
- teacher_audio: bfloat16 [16384, 512], P('wide'), may hold values from -16 to 16
- teacher_text: bfloat16 [16384, 512], P(('wide', 'mp')), may hold values from -16 to 16
- w_first: bfloat16 [768, 512], P(None, 'mp'), may hold values from -0.21875 to 0.21875
- w_second: bfloat16 [512, 512], P('mp'), may hold values from -0.25 to 0.25
- pairing: int32 [16384], P('wide'), may hold values from 0 to 16383
Outputs:
- loss: float32 [], replicated
- grad_first: float32 [768, 512], P(None, 'mp')
- grad_second: float32 [512, 512], P('mp')
The draws below stay inside these ranges and needn't reach their ends.
All inputs are finite; a program needn't handle non-finite values.
Results may differ from the reference program's by a relative error of at most 0.0052.
Values may be sent and summed in bfloat16 or wider, within the bound.
A program may use at most 64 MiB of HBM per device.

```python
import math
import jax
import jax.numpy as jnp
from jax import lax

D_AUDIO = 768
HIDDEN_UNITS = 512
EMBED = 512
ROWS_DEV = 128
BATCH = 16384


def unit_rows(values):
    return values / jnp.sqrt(jnp.sum(values * values, axis=1, keepdims=True))


def pair_index(key):
    return jax.random.randint(jax.random.fold_in(key, 11), (BATCH,), 0, BATCH, dtype=jnp.int32)


def caption_directions(key):
    groups = max(2, BATCH // 256)
    member = jax.random.randint(jax.random.fold_in(key, 12), (BATCH,), 0, groups, dtype=jnp.int32)
    centers = unit_rows(jax.random.normal(jax.random.fold_in(key, 13), (groups, EMBED), jnp.float32))
    pull = jax.random.uniform(jax.random.fold_in(key, 15), (groups,), jnp.float32, 0.55, 0.9)
    noise = unit_rows(jax.random.normal(jax.random.fold_in(key, 16), (BATCH, EMBED), jnp.float32))
    own_center = jnp.take(centers, member, axis=0)
    own_pull = jnp.take(pull, member, axis=0)[:, None]
    mixed = own_pull * own_center + jnp.sqrt(1.0 - own_pull * own_pull) * noise
    return unit_rows(mixed)


def row_scales(key, scale_low, scale_high):
    return jnp.exp(jax.random.uniform(key, (BATCH, 1), jnp.float32, math.log(scale_low), math.log(scale_high)))


def draw_pairing(key, part):
    return pair_index(key)


def draw_teacher_text(key, part):
    scale_low = 0.3
    scale_high = 3.0
    directions = caption_directions(key)
    scales = row_scales(jax.random.fold_in(key, 31), scale_low, scale_high)
    return jnp.clip(directions * scales * math.sqrt(float(EMBED)), -16.0, 16.0).astype(jnp.bfloat16)


def draw_teacher_audio(key, part):
    align_low = 0.3
    align_high = 0.9
    scale_low = 0.3
    scale_high = 3.0
    directions = caption_directions(key)
    paired = jnp.take(directions, pair_index(key), axis=0)
    align = jnp.exp(jax.random.uniform(jax.random.fold_in(key, 41), (BATCH, 1), jnp.float32, math.log(align_low), math.log(align_high)))
    noise = unit_rows(jax.random.normal(jax.random.fold_in(key, 42), (BATCH, EMBED), jnp.float32))
    mixed = unit_rows(align * paired + jnp.sqrt(1.0 - align * align) * noise)
    scales = row_scales(jax.random.fold_in(key, 43), scale_low, scale_high)
    return jnp.clip(mixed * scales * math.sqrt(float(EMBED)), -16.0, 16.0).astype(jnp.bfloat16)


def shard_levels(own_key, shape, split, low, top_value):
    def one(axis_at, blocks):
        draws = jax.random.uniform(jax.random.fold_in(jax.random.fold_in(own_key, 6), axis_at), (blocks,), jnp.float32, low / len(split), top_value / len(split))
        return jnp.repeat(jnp.exp(draws), shape[axis_at] // blocks).reshape((-1,) + (1,) * (len(shape) - axis_at - 1))

    gain = one(*split[0])
    for cut in split[1:]:
        gain = gain * one(*cut)
    return gain


def gaussian(stream_key, extent, scale, limit, split=(), kind=jnp.bfloat16):
    level = shard_levels(stream_key, extent, split, -0.22, 0.18) if split else 1.0
    drawn = jax.random.normal(stream_key, extent, jnp.float32) * scale * level
    return jnp.minimum(jnp.maximum(drawn, -limit), limit).astype(kind)


def setup_inputs(seed: int = 0) -> dict:
    key_list = jax.random.split(jax.random.key(seed), 7)
    clip_feats = gaussian(key_list[0], (BATCH, D_AUDIO), 1.0, 6.0, ((0, 128),))
    teacher_audio = draw_teacher_audio(jax.random.fold_in(key_list[6], 71), 0)
    teacher_text = draw_teacher_text(jax.random.fold_in(key_list[6], 71), 0)
    w_first = gaussian(key_list[3], (D_AUDIO, HIDDEN_UNITS), D_AUDIO ** -0.5, 0.21875, ((1, 4),))
    w_second = gaussian(key_list[4], (HIDDEN_UNITS, EMBED), HIDDEN_UNITS ** -0.5, 0.25, ((0, 4),))
    pairing = draw_pairing(jax.random.fold_in(key_list[6], 71), 0)
    return dict(clip_feats=clip_feats, teacher_audio=teacher_audio, teacher_text=teacher_text, w_first=w_first, w_second=w_second, pairing=pairing)


teacher_scale = 14.0
student_scale = 64.0
eps = 1e-06

def normalize(values):
    return values / jnp.sqrt(lax.optimization_barrier(jnp.sum(values * values, axis=1, keepdims=True)) + eps)

def inner_rows(left, right):
    return lax.dot_general(left, right, (((1,), (1,)), ((), ())), preferred_element_type=jnp.float32)

def reference(clip_feats, teacher_audio, teacher_text, w_first, w_second, pairing):
    total = clip_feats.shape[0]
    pre_act = jnp.dot(clip_feats, w_first, preferred_element_type=jnp.float32)
    gelu_out, gelu_back = jax.vjp(lambda u: jax.nn.gelu(u, approximate=False), pre_act)
    hidden = gelu_out.astype(jnp.bfloat16)
    raw = jnp.dot(hidden, w_second, preferred_element_type=jnp.float32)
    norm = jnp.sqrt(lax.optimization_barrier(jnp.sum(raw * raw, axis=1, keepdims=True)) + eps)
    student = raw / norm
    stud_b = student.astype(jnp.bfloat16)
    teach_b = normalize(teacher_audio.astype(jnp.float32)).astype(jnp.bfloat16)
    capt_b = normalize(teacher_text.astype(jnp.float32)).astype(jnp.bfloat16)
    column_ids = jnp.arange(total, dtype=jnp.int32)

    def block_work(operands):
        teach_blk, stud_blk, pair_blk = operands
        tlog = teacher_scale * inner_rows(teach_blk, capt_b)
        slog = student_scale * inner_rows(stud_blk, capt_b)
        texp = jnp.exp(tlog)
        sexp = jnp.exp(slog)
        zt_sum = lax.optimization_barrier(jnp.sum(texp, axis=1))
        zs_sum = lax.optimization_barrier(jnp.sum(sexp, axis=1))
        acc_sum = lax.optimization_barrier(jnp.sum(texp * (tlog - slog), axis=1))
        hit = column_ids[None, :] == pair_blk[:, None]
        spair = lax.optimization_barrier(jnp.sum(jnp.where(hit, slog, 0.0), axis=1))
        loss_blk = jnp.sum(acc_sum / zt_sum - jnp.log(zt_sum) + 2.0 * jnp.log(zs_sum) - spair)
        coef = (2.0 * sexp / zs_sum[:, None] - texp / zt_sum[:, None] - hit.astype(jnp.float32)).astype(jnp.bfloat16)
        dstud = jnp.dot(coef, capt_b, preferred_element_type=jnp.float32)
        return (loss_blk, dstud)
    block_rows = ROWS_DEV
    loss_parts, dstud = lax.map(block_work, (teach_b.reshape(-1, block_rows, EMBED), stud_b.reshape(-1, block_rows, EMBED), pairing.reshape(-1, block_rows)))
    loss = jnp.sum(loss_parts) / total
    dstud = dstud.reshape(total, EMBED) * (student_scale / total)
    draw = ((dstud - student * lax.optimization_barrier(jnp.sum(student * dstud, axis=1, keepdims=True))) / norm).astype(jnp.bfloat16)
    grad_second = jnp.dot(hidden.T, draw, preferred_element_type=jnp.float32)
    dhid = jnp.dot(draw, w_second.T, preferred_element_type=jnp.float32)
    dpre = gelu_back(dhid)[0].astype(jnp.bfloat16)
    grad_first = jnp.dot(clip_feats.T, dpre, preferred_element_type=jnp.float32)
    return (loss, grad_first, grad_second)
```

```python
import jax
import jax.numpy as jnp
from jax import lax
from jax.experimental import pallas as pl
from jax.experimental.pallas import tpu as pltpu
from jax.sharding import Mesh
from jax.sharding import PartitionSpec as P

MESH = pl.DeviceIdType.MESH
WIDE = ("y", "z", "xl")
F32 = jnp.float32
BF16 = jnp.bfloat16

Y, Z, XL, MP = 4, 16, 2, 4
LINE = XL * MP
TEACHER_SCALE = 14.0
STUDENT_SCALE = 64.0
EPS = 1e-6
TILES = 10


def dot_nt(left, right, precision=None):
    return lax.dot_general(
        left, right, (((1,), (1,)), ((), ())), preferred_element_type=F32, precision=precision
    )


def normalize(values):
    return values / jnp.sqrt(jnp.sum(values * values, axis=1, keepdims=True) + EPS)


def rows(start, size):
    return pl.ds(pl.multiple_of(start, size), size)


def kernel(
    clip_h, ta_h, tt_h, w1_h, w2_h, pair_h,
    loss_o, gf_o, gs_o,
    clip_v, ta_v, tt_v, w1_v, w2_v, pair_v,
    A, B, C, stk, prow, pcol, rawp, rawr, st32, nm32, gprime, hid_v,
    ET, ES, acc, stat, statr, dp, dpb, rsr, drw,
    lossy, lossyr, lossz, losszr,
    gsb, gfb, p1s, p1f, own1, T, p2r, R, RR,
    sem_in, sA, rA, sB, rB, sB0, rB0, sC, rC,
    s_raw, r_raw, s_stud, r_stud, s_tp, r_tp, s_stat, r_stat, s_rs, r_rs, s_dr, r_dr,
    s_ly, r_ly, s_lz, r_lz, s_p1, r_p1, s_p2, r_p2, s_p3, r_p3, s_p4, r_p4,
):
    y, z = lax.axis_index("y"), lax.axis_index("z")
    xl, mp = lax.axis_index("xl"), lax.axis_index("mp")
    q = xl * MP + mp
    j = y * XL + xl
    total = 128 * Y * Z * XL

    def rem(v, n):
        return lax.rem(v + 4 * n, n)

    def y_peer(e):
        return (rem(y + e, Y), z, xl, mp)

    def z_peer(e):
        return (y, rem(z + e, Z), xl, mp)

    def line_peer(e):
        other = rem(q + e, LINE)
        return (y, z, other // MP, rem(other, MP))

    def mp_peer(e):
        return (y, z, xl, rem(mp + e, MP))

    def group_peer(e):
        other = rem(j + e, Y * XL)
        return (other // XL, z, rem(other, XL), mp)

    def remote(src, dst, send, recv, to):
        return pltpu.make_async_remote_copy(
            src_ref=src, dst_ref=dst, send_sem=send, recv_sem=recv, device_id=to,
            device_id_type=MESH,
        )

    me = (y, z, xl, mp)
    sends = []

    def push(*args):
        copy = remote(*args)
        copy.start()
        sends.append(copy)

    def arrived(dst, recv):
        remote(dst, dst, recv, recv, me).wait_recv()

    ins = [
        pltpu.make_async_copy(h, v, sem_in.at[i])
        for i, (h, v) in enumerate(
            [(tt_h, tt_v), (clip_h, clip_v), (w1_h, w1_v), (w2_h, w2_v), (ta_h, ta_v), (pair_h, pair_v)]
        )
    ]
    for c in ins:
        c.start()
    barrier = pltpu.get_barrier_semaphore()
    partners = [line_peer(e) for e in range(1, LINE)]
    partners += [y_peer(e) for e in range(1, Y)] + [z_peer(1), z_peer(-1)]
    for p in partners:
        pl.semaphore_signal(barrier, inc=1, device_id=p, device_id_type=MESH)
    ins[0].wait()
    A[0, 0] = normalize(tt_v[...].astype(F32)).astype(BF16)
    pl.semaphore_wait(barrier, len(partners))

    for e in (1, 3, 2):
        push(A.at[0, 0, pl.ds(0, 16)], B.at[0, 0, 3 - e], sB0.at[3 - e], rB0.at[3 - e], y_peer(e))
    push(A.at[0, 0], A.at[1, 0], sA.at[1, 0], rA.at[1, 0], z_peer(1))
    push(A.at[0, 0], A.at[1, 1], sA.at[1, 1], rA.at[1, 1], z_peer(-1))
    for e in (1, 3, 2):
        push(A.at[0, 0, pl.ds(16, 16)], C.at[0, 3 - e, 0], sC.at[0, 3 - e], rC.at[0, 3 - e], y_peer(e))

    for c in ins[1:4]:
        c.wait()
    pre = jnp.dot(clip_v[...], w1_v[...], preferred_element_type=F32)
    cdf = 0.5 * (1.0 + lax.erf(pre * 0.7071067811865476))
    hid = (pre * cdf).astype(BF16)
    hid_v[...] = hid
    rawp[...] = jnp.dot(hid, w2_v[...], preferred_element_type=F32)
    for e in (2, 1, 3):
        other = rem(mp + e, MP)
        push(rawp.at[rows(other * 32, 32)], rawr.at[e - 1], s_raw.at[e - 1], r_raw.at[e - 1], mp_peer(e))
    for e in range(1, Y):
        arrived(B.at[0, 0, 3 - e], rB0.at[3 - e])
    push(B.at[0, 0], B.at[1, 0], sB.at[1, 0], rB.at[1, 0], z_peer(1))
    push(B.at[0, 0], B.at[1, 1], sB.at[1, 1], rB.at[1, 1], z_peer(-1))
    ins[4].wait()
    ins[5].wait()
    mine = rows(xl * 128, 128)
    stk[mine] = normalize(ta_v[...].astype(F32)).astype(BF16)
    prow[xl] = jnp.broadcast_to(pair_v[...], (8, 128))
    other_x = (y, z, 1 - xl, mp)
    push(stk.at[mine], stk.at[mine], s_tp.at[0], r_tp.at[0], other_x)
    push(prow.at[xl], prow.at[xl], s_tp.at[1], r_tp.at[1], other_x)
    gprime[...] = cdf + pre * (0.3989422804014327 * jnp.exp(-0.5 * pre * pre))

    def comm(k):
        for d, way in ((0, 1), (1, -1)):
            arrived(A.at[k, d], rA.at[k, d])
            if k < 7:
                push(A.at[k, d], A.at[k + 1, d], sA.at[k + 1, d], rA.at[k + 1, d], z_peer(way))
            elif d == 0:
                push(A.at[k, d], A.at[0, 1], sA.at[0, 1], rA.at[0, 1], z_peer(way))
        for e in (1, 3, 2):
            push(
                A.at[k, :, pl.ds(16, 16)], C.at[k, 3 - e], sC.at[k, 3 - e], rC.at[k, 3 - e],
                y_peer(e),
            )
        for d, way in ((0, 1), (1, -1)):
            arrived(B.at[k, d], rB.at[k, d])
            if k < 7:
                push(B.at[k, d], B.at[k + 1, d], sB.at[k + 1, d], rB.at[k + 1, d], z_peer(way))
            elif d == 1:
                push(B.at[k, d], B.at[0, 1], sB.at[0, 1], rB.at[0, 1], z_peer(way))

    def far():
        arrived(A.at[0, 1], rA.at[0, 1])
        for e in (1, 3, 2):
            push(
                A.at[0, 1, pl.ds(16, 16)], C.at[0, 3 - e, 1], sC.at[8, 3 - e], rC.at[8, 3 - e],
                y_peer(e),
            )
        arrived(B.at[0, 1], rB.at[0, 1])

    col = lax.broadcasted_iota(jnp.int32, (8, 256), 1)
    in_a, in_b = col < 64, col < 160
    b_way = (col >= 112).astype(jnp.int32)
    b_at = col - 64 - 48 * b_way
    b_off = 1 + (b_at >= 16).astype(jnp.int32) + (b_at >= 32).astype(jnp.int32)
    c_at = col - 160
    c_off = 1 + (c_at >= 32).astype(jnp.int32) + (c_at >= 64).astype(jnp.int32)
    way = jnp.where(in_a, (col >= 32).astype(jnp.int32), jnp.where(in_b, b_way, (c_at & 16) // 16))
    y_off = jnp.where(in_a, 0, jnp.where(in_b, b_off, c_off))
    line = jnp.where(in_a, col & 31, jnp.where(in_b, b_at & 15, 16 + (c_at & 15)))
    y_at = (y + y_off) & (Y - 1)
    id_base = ((y_at * Z) * XL + xl) * 128 + mp * 32 + line

    def hits(k):
        z_left = rem(z - k, Z)
        z_right = jnp.where(k == 0, rem(z + 8, Z), rem(z + k, Z))
        ids = id_base + jnp.where(way == 1, z_right, z_left) * (XL * 128)
        ids = ids[0:1].astype(F32)
        return [pcol[...] == ids[:, h * 128 : (h + 1) * 128] for h in (0, 1)]

    def captions(k):
        return jnp.concatenate(
            [A[k].reshape(64, 512), B[k].reshape(96, 512), C[k].reshape(96, 512)], axis=0
        )

    def chunk(k):
        scores = dot_nt(stk[...], captions(k))
        tlog = TEACHER_SCALE * scores[:256]
        slog = STUDENT_SCALE * scores[256:]
        texp, sexp = jnp.exp(tlog), jnp.exp(slog)
        ET[k] = texp
        ES[k] = sexp
        lean = texp * (tlog - slog)
        hit = hits(k)
        pair = [jnp.where(hit[h], slog[:, h * 128 : (h + 1) * 128], 0.0) for h in (0, 1)]
        acc[0] += texp[:, :128] + texp[:, 128:]
        acc[1] += sexp[:, :128] + sexp[:, 128:]
        acc[2] += lean[:, :128] + lean[:, 128:]
        acc[3] += pair[0] + pair[1]

    def c_arrived(k):
        for d in range(3):
            arrived(C.at[k, d], rC.at[k, d])

    acc[...] = jnp.zeros_like(acc)
    comm(1)
    for e in range(1, MP):
        arrived(rawr.at[e - 1], r_raw.at[e - 1])
    raw = rawp[rows(mp * 32, 32)] + rawr[0] + rawr[1] + rawr[2]
    norm = jnp.sqrt(jnp.sum(raw * raw, axis=1, keepdims=True) + EPS)
    student = raw / norm
    st32[...] = student
    nm32[...] = jnp.broadcast_to(norm, (32, 128))
    own = rows(256 + q * 32, 32)
    stk[own] = student.astype(BF16)
    for e in range(1, LINE):
        push(stk.at[own], stk.at[own], s_stud.at[e - 1], r_stud.at[e - 1], line_peer(e))
    comm(2)
    theirs = rows((1 - xl) * 128, 128)
    arrived(stk.at[theirs], r_tp.at[0])
    arrived(prow.at[1 - xl], r_tp.at[1])
    for i in range(XL):
        one = jnp.broadcast_to(prow[i][0:1].astype(F32), (128, 128))
        pcol[pl.ds(i * 128, 128)] = one.T
    comm(3)
    for e in range(1, LINE):
        arrived(stk.at[rows(256 + rem(q - e, LINE) * 32, 32)], r_stud.at[e - 1])
    for k in range(4, 8):
        comm(k)
        c_arrived(k - 3)
        chunk(k - 3)
    far()
    for k in range(5, 8):
        c_arrived(k)
        chunk(k)
    for d in range(3):
        arrived(C.at[0, d, 0], rC.at[0, d])
        arrived(C.at[0, d, 1], rC.at[8, d])
    chunk(0)

    pick = (
        lax.broadcasted_iota(jnp.int32, (8, 512), 0)
        == lax.broadcasted_iota(jnp.int32, (8, 512), 1) // 128
    ).astype(F32)
    stat[...] = dot_nt(
        pick, jnp.concatenate([acc[i] for i in range(4)], axis=1), lax.Precision.HIGHEST
    )
    for e in range(1, LINE):
        push(stat, statr.at[e - 1], s_stat.at[e - 1], r_stat.at[e - 1], line_peer(e))
    for e in range(1, LINE):
        arrived(statr.at[e - 1], r_stat.at[e - 1])
    sums = stat[...]
    for e in range(1, LINE):
        sums = sums + statr[e - 1]
    zt, zs, lean, pair = (sums[i : i + 1] for i in range(4))
    part = jnp.sum(lean / zt - jnp.log(zt) + 2.0 * jnp.log(zs) - pair, axis=1, keepdims=True)
    lossy[...] = jnp.broadcast_to(part, (8, 128))
    for e in range(1, Y):
        push(lossy, lossyr.at[e - 1], s_ly.at[e - 1], r_ly.at[e - 1], y_peer(e))
    c_t = jnp.broadcast_to(1.0 / zt, (128, 256)).T
    c_s = jnp.broadcast_to(2.0 / zs, (128, 256)).T

    for k in range(8):
        hit = hits(k)
        coef = jnp.concatenate(
            [
                (
                    ES[k, :, h * 128 : (h + 1) * 128] * c_s
                    - ET[k, :, h * 128 : (h + 1) * 128] * c_t
                    - hit[h].astype(F32)
                ).astype(BF16)
                for h in (0, 1)
            ],
            axis=1,
        )
        more = jnp.dot(coef, captions(k), preferred_element_type=F32)
        if k == 0:
            dp[...] = more
        else:
            dp[...] += more
    dpb[...] = dp[...].astype(BF16)
    for e in (3, 5, 4, 1, 7, 2, 6):
        other = rem(q + e, LINE)
        push(dpb.at[rows(other * 32, 32)], rsr.at[e - 1], s_rs.at[e - 1], r_rs.at[e - 1], line_peer(e))
    for e in range(1, Y):
        arrived(lossyr.at[e - 1], r_ly.at[e - 1])
    lossz[...] = lossy[...] + lossyr[0] + lossyr[1] + lossyr[2]
    for e in range(1, Z):
        push(lossz, losszr.at[e - 1], s_lz.at[e - 1], r_lz.at[e - 1], z_peer(e))
    dstud = dp[rows(q * 32, 32)]
    for e in range(1, LINE):
        arrived(rsr.at[e - 1], r_rs.at[e - 1])
        dstud = dstud + rsr[e - 1].astype(F32)
    dstud = dstud * (STUDENT_SCALE / total)
    student = st32[...]
    inner = jnp.sum(student * dstud, axis=1, keepdims=True)
    own = rows(mp * 32, 32)
    drw[own] = ((dstud - student * inner) / nm32[:, 0:1]).astype(BF16)
    for e in (2, 1, 3):
        push(drw.at[own], drw.at[own], s_dr.at[e - 1], r_dr.at[e - 1], mp_peer(e))
    for e in range(1, MP):
        arrived(drw.at[rows(rem(mp - e, MP) * 32, 32)], r_dr.at[e - 1])

    draw = drw[...]
    gs = lax.dot_general(
        hid_v[...], draw, (((0,), (0,)), ((), ())), preferred_element_type=F32
    )
    gsb[...] = gs.astype(BF16)
    group = Y * XL
    for e in range(1, group):
        other = rem(j + e, group)
        push(gsb.at[rows(other * 16, 16)], p1s.at[e - 1], s_p1.at[0, e - 1], r_p1.at[0, e - 1], group_peer(e))
    gs_o[...] = gs
    dpre = (dot_nt(draw, w2_v[...]) * gprime[...]).astype(BF16)
    gf = lax.dot_general(
        clip_v[...], dpre, (((0,), (0,)), ((), ())), preferred_element_type=F32
    )
    gfb[...] = gf.astype(BF16)
    for e in range(1, group):
        other = rem(j + e, group)
        push(gfb.at[rows(other * 96, 96)], p1f.at[e - 1], s_p1.at[1, e - 1], r_p1.at[1, e - 1], group_peer(e))
    gf_o[...] = gf
    one_s = gs_o[rows(j * 16, 16)]
    one_f = gf_o[rows(j * 96, 96)]
    for e in range(1, group):
        arrived(p1s.at[e - 1], r_p1.at[0, e - 1])
        one_s = one_s + p1s[e - 1].astype(F32)
    for e in range(1, group):
        arrived(p1f.at[e - 1], r_p1.at[1, e - 1])
        one_f = one_f + p1f[e - 1].astype(F32)
    own1[pl.ds(0, 96)] = one_f
    for i in range(4):
        own1[pl.ds(96 + 16 * i, 16)] = one_s[:, i * 128 : (i + 1) * 128]
    T[...] = own1[...].astype(BF16)
    for t in range(TILES):

        @pl.when(z != t)
        def _():
            slot = rem(z - t, Z) - 1
            remote(
                T.at[pl.ds(16 * t, 16)], p2r.at[slot], s_p2.at[t], r_p2.at[slot], (y, t, xl, mp)
            ).start()

    loss_sum = lossz[...]
    for e in range(1, Z):
        arrived(losszr.at[e - 1], r_lz.at[e - 1])
        loss_sum = loss_sum + losszr[e - 1]
    loss_o[0, 0] = jnp.sum(loss_sum[0:1, 0:1]) / total

    @pl.when(z < TILES)
    def _():
        tile = rows(z * 16, 16)
        out = own1[tile]
        for e in range(1, Z):
            arrived(p2r.at[e - 1], r_p2.at[e - 1])
            out = out + p2r[e - 1].astype(F32)
        R[tile] = out.astype(BF16)
        for e in range(1, Z):
            remote(R.at[tile], R.at[tile], s_p3.at[e - 1], r_p3.at[z], z_peer(e)).start()

    for t in range(TILES):

        @pl.when(z != t)
        def _():
            arrived(R.at[pl.ds(16 * t, 16)], r_p3.at[t])

    for e in range(1, group):
        push(R, RR.at[e - 1], s_p4.at[e - 1], r_p4.at[e - 1], group_peer(e))

    def write(owner, ref):
        gf_o[rows(owner * 96, 96)] = ref[pl.ds(0, 96)].astype(F32)
        for i in range(4):
            gs_o[rows(owner * 16, 16), i * 128 : (i + 1) * 128] = ref[
                pl.ds(96 + 16 * i, 16)
            ].astype(F32)

    write(j, R)
    for e in range(1, group):
        arrived(RR.at[e - 1], r_p4.at[e - 1])
        write(rem(j - e, group), RR.at[e - 1])

    for copy in sends:
        copy.wait_send()
    for t in range(TILES):

        @pl.when(z != t)
        def _():
            remote(T.at[pl.ds(16 * t, 16)], T.at[pl.ds(16 * t, 16)], s_p2.at[t], s_p2.at[t], me).wait_send()

    @pl.when(z < TILES)
    def _():
        tile = rows(z * 16, 16)
        for e in range(1, Z):
            remote(R.at[tile], R.at[tile], s_p3.at[e - 1], s_p3.at[e - 1], me).wait_send()


def body(clip_feats, teacher_audio, teacher_text, w_first, w_second, pairing):
    vm = pltpu.VMEM
    dma = pltpu.SemaphoreType.DMA
    hbm = pl.BlockSpec(memory_space=pl.ANY)
    scratch = [
        vm((128, 768), BF16), vm((128, 512), BF16), vm((32, 512), BF16),
        vm((768, 128), BF16), vm((128, 512), BF16), vm((1, 128), jnp.int32),
        vm((8, 2, 32, 512), BF16), vm((8, 2, 3, 16, 512), BF16), vm((8, 3, 2, 16, 512), BF16),
        vm((512, 512), BF16), vm((2, 8, 128), jnp.int32), vm((256, 128), F32),
        vm((128, 512), F32), vm((3, 32, 512), F32), vm((32, 512), F32), vm((32, 128), F32),
        vm((128, 128), F32), vm((128, 128), BF16),
        vm((8, 256, 256), F32), vm((8, 256, 256), F32), vm((4, 256, 128), F32),
        vm((8, 256), F32), vm((7, 8, 256), F32),
        vm((256, 512), F32), vm((256, 512), BF16), vm((7, 32, 512), BF16), vm((128, 512), BF16),
        vm((8, 128), F32), vm((3, 8, 128), F32), vm((8, 128), F32), vm((15, 8, 128), F32),
        vm((128, 512), BF16), vm((768, 128), BF16), vm((7, 16, 512), BF16), vm((7, 96, 128), BF16),
        vm((160, 128), F32), vm((160, 128), BF16), vm((15, 16, 128), BF16),
        vm((160, 128), BF16), vm((7, 160, 128), BF16),
        dma((6,)), dma((8, 2)), dma((8, 2)), dma((8, 2)), dma((8, 2)), dma((3,)), dma((3,)),
        dma((9, 3)), dma((9, 3)),
        dma((3,)), dma((3,)), dma((7,)), dma((7,)), dma((2,)), dma((2,)), dma((7,)), dma((7,)),
        dma((7,)), dma((7,)), dma((3,)), dma((3,)),
        dma((3,)), dma((3,)), dma((15,)), dma((15,)), dma((2, 7)), dma((2, 7)),
        dma((TILES,)), dma((15,)), dma((15,)), dma((TILES,)), dma((7,)), dma((7,)),
    ]
    loss, grad_first, grad_second = pl.pallas_call(
        kernel,
        out_shape=(
            jax.ShapeDtypeStruct((1, 1), F32),
            jax.ShapeDtypeStruct((768, 128), F32),
            jax.ShapeDtypeStruct((128, 512), F32),
        ),
        in_specs=[hbm] * 6,
        out_specs=(
            pl.BlockSpec(memory_space=pltpu.SMEM),
            pl.BlockSpec(memory_space=pltpu.VMEM),
            pl.BlockSpec(memory_space=pltpu.VMEM),
        ),
        scratch_shapes=scratch,
        compiler_params=pltpu.CompilerParams(
            collective_id=0, has_side_effects=True, vmem_limit_bytes=48 * 1024 * 1024
        ),
    )(clip_feats, teacher_audio, teacher_text, w_first, w_second, pairing.reshape(1, 128))
    return loss.reshape(()), grad_first, grad_second


def solution(mesh):
    finer = Mesh(mesh.devices.reshape(Y, Z, XL, MP), ("y", "z", "xl", "mp"))
    return jax.shard_map(
        body,
        mesh=finer,
        in_specs=(
            P(WIDE, None),
            P(WIDE, None),
            P(WIDE + ("mp",), None),
            P(None, "mp"),
            P("mp", None),
            P(WIDE),
        ),
        out_specs=(P(), P(None, "mp"), P("mp", None)),
        check_vma=False,
    )
```

```python
import jax
import jax.numpy as jnp
from jax import lax
from jax.experimental import pallas as pl
from jax.experimental.pallas import tpu as pltpu
from jax.sharding import Mesh
from jax.sharding import PartitionSpec as P

MESH = pl.DeviceIdType.MESH
WIDE = ("y", "z", "xl")
F32 = jnp.float32
BF16 = jnp.bfloat16

Y, Z, XL, MP = 4, 16, 2, 4
LINE = XL * MP
TEACHER_SCALE = 14.0
STUDENT_SCALE = 64.0
EPS = 1e-6
TILES = 10


def dot_nt(left, right):
    return lax.dot_general(
        left, right, (((1,), (1,)), ((), ())), preferred_element_type=F32
    )


def normalize(values):
    return values / jnp.sqrt(jnp.sum(values * values, axis=1, keepdims=True) + EPS)


def rows(start, size):
    return pl.ds(pl.multiple_of(start, size), size)


def kernel(
    clip_h, ta_h, tt_h, w1_h, w2_h, pair_h,
    loss_o, gf_o, gs_o,
    clip_v, ta_v, tt_v, w1_v, w2_v, pair_v,
    G, stk, prow, pcol, rawp, rawr, st32, nm32, gprime, hid_v,
    ET, ES, acc, stat, statr, dp, dpb, rsr, drw,
    lossy, lossyr, lossz, losszr,
    gsb, gfb, p1s, p1f, own1, T, p2r, R, RR,
    sem_in, sA, rA, sB, rB, sC, rC,
    s_raw, r_raw, s_stud, r_stud, s_tp, r_tp, s_stat, r_stat, s_rs, r_rs, s_dr, r_dr,
    s_ly, r_ly, s_lz, r_lz, s_p1, r_p1, s_p2, r_p2, s_p3, r_p3, s_p4, r_p4,
):
    y, z = lax.axis_index("y"), lax.axis_index("z")
    xl, mp = lax.axis_index("xl"), lax.axis_index("mp")
    q = xl * MP + mp
    j = y * XL + xl
    total = 128 * Y * Z * XL

    def rem(v, n):
        return lax.rem(v + 4 * n, n)

    def y_peer(e):
        return (rem(y + e, Y), z, xl, mp)

    def z_peer(e):
        return (y, rem(z + e, Z), xl, mp)

    def line_peer(e):
        other = rem(q + e, LINE)
        return (y, z, other // MP, rem(other, MP))

    def mp_peer(e):
        return (y, z, xl, rem(mp + e, MP))

    def group_peer(e):
        other = rem(j + e, Y * XL)
        return (other // XL, z, rem(other, XL), mp)

    def remote(src, dst, send, recv, to):
        return pltpu.make_async_remote_copy(
            src_ref=src, dst_ref=dst, send_sem=send, recv_sem=recv, device_id=to,
            device_id_type=MESH,
        )

    me = (y, z, xl, mp)
    sends = []

    def push(*args):
        copy = remote(*args)
        copy.start()
        sends.append(copy)

    def arrived(dst, recv):
        remote(dst, dst, recv, recv, me).wait_recv()

    ins = [
        pltpu.make_async_copy(h, v, sem_in.at[i])
        for i, (h, v) in enumerate(
            [(tt_h, tt_v), (clip_h, clip_v), (w1_h, w1_v), (w2_h, w2_v), (ta_h, ta_v), (pair_h, pair_v)]
        )
    ]
    for c in ins:
        c.start()
    barrier = pltpu.get_barrier_semaphore()
    partners = [line_peer(e) for e in range(1, LINE)]
    partners += [y_peer(e) for e in range(1, Y)] + [z_peer(e) for e in (1, -1, 2, -2)]
    for p in partners:
        pl.semaphore_signal(barrier, inc=1, device_id=p, device_id_type=MESH)
    ins[0].wait()
    G[0, 0, 0] = normalize(tt_v[...].astype(F32)).astype(BF16)
    pl.semaphore_wait(barrier, len(partners))

    def along_z(o, k, d, send, recv):
        way = 1 - 2 * d
        for step in (2, 1):
            slot, side = k + step, d
            if slot == 8:
                if d != o // 2:
                    continue
                slot, side = 0, 1
            src = G.at[k, o, 0 if k == 0 else d]
            push(src, G.at[slot, o, side], send.at[slot, side], recv.at[slot, side], z_peer(way * step))

    def along_y(k, d):
        for e in (1, 3):
            push(G.at[k, 0, d], G.at[k, Y - e, d], sC.at[k, d, e // 2], rC.at[k, d, e // 2], y_peer(e))

    push(G.at[0, 0, 0], G.at[0, 2, 0], sB.at[0, 0], rB.at[0, 0], y_peer(2))
    for d in (0, 1):
        along_z(0, 0, d, sA, rA)
    along_y(0, 0)

    for c in ins[1:4]:
        c.wait()
    pre = jnp.dot(clip_v[...], w1_v[...], preferred_element_type=F32)
    cdf = 0.5 * (1.0 + lax.erf(pre * 0.7071067811865476))
    hid = (pre * cdf).astype(BF16)
    hid_v[...] = hid
    rawp[...] = jnp.dot(hid, w2_v[...], preferred_element_type=F32)
    for e in (2, 1, 3):
        other = rem(mp + e, MP)
        push(rawp.at[rows(other * 32, 32)], rawr.at[e - 1], s_raw.at[e - 1], r_raw.at[e - 1], mp_peer(e))
    arrived(G.at[0, 2, 0], rB.at[0, 0])
    for d in (0, 1):
        along_z(2, 0, d, sB, rB)
    ins[4].wait()
    ins[5].wait()
    mine = rows(xl * 128, 128)
    stk[mine] = normalize(ta_v[...].astype(F32)).astype(BF16)
    prow[xl] = jnp.broadcast_to(pair_v[...], (8, 128))
    other_x = (y, z, 1 - xl, mp)
    push(stk.at[mine], stk.at[mine], s_tp.at[0], r_tp.at[0], other_x)
    push(prow.at[xl], prow.at[xl], s_tp.at[1], r_tp.at[1], other_x)
    gprime[...] = cdf + pre * (0.3989422804014327 * jnp.exp(-0.5 * pre * pre))

    def comm(k):
        for d in (0, 1):
            arrived(G.at[k, 0, d], rA.at[k, d])
            along_z(0, k, d, sA, rA)
        for d in (0, 1):
            arrived(G.at[k, 2, d], rB.at[k, d])
            along_z(2, k, d, sB, rB)
        for d in (0, 1):
            arrived(G.at[k - 1, 0, d], rA.at[k - 1, d])
            along_y(k - 1, d)
            along_y(k, d)

    def far():
        for k, d in ((7, 0), (7, 1), (0, 1)):
            arrived(G.at[k, 0, d], rA.at[k, d])
            along_y(k, d)

    col = lax.broadcasted_iota(jnp.int32, (8, 256), 1)
    way = (col // 32) & 1
    y_at = (y + col // 64) & (Y - 1)
    id_base = ((y_at * Z) * XL + xl) * 128 + mp * 32 + (col & 31)

    def hits(k):
        z_left = rem(z - k, Z)
        z_right = jnp.where(k == 0, rem(z + 8, Z), rem(z + k, Z))
        ids = id_base + jnp.where(way == 1, z_right, z_left) * (XL * 128)
        ids = ids[0:1].astype(F32)
        return [pcol[...] == ids[:, h * 128 : (h + 1) * 128] for h in (0, 1)]

    def captions(k):
        return G[k].reshape(256, 512)

    def chunk(k):
        scores = dot_nt(stk[...], captions(k))
        tlog = TEACHER_SCALE * scores[:256]
        slog = STUDENT_SCALE * scores[256:]
        texp, sexp = jnp.exp(tlog), jnp.exp(slog)
        ET[k] = texp
        ES[k] = sexp
        lean = texp * (tlog - slog)
        hit = hits(k)
        pair = [jnp.where(hit[h], slog[:, h * 128 : (h + 1) * 128], 0.0) for h in (0, 1)]
        acc[0] += texp[:, :128] + texp[:, 128:]
        acc[1] += sexp[:, :128] + sexp[:, 128:]
        acc[2] += lean[:, :128] + lean[:, 128:]
        acc[3] += pair[0] + pair[1]

    def complete(k):
        for d in (0, 1):
            if k == 7 or (k in (1, 3, 5)) or (k == 0 and d == 1):
                arrived(G.at[k, 2, d], rB.at[k, d])
            for e in (1, 3):
                arrived(G.at[k, Y - e, d], rC.at[k, d, e // 2])

    acc[...] = jnp.zeros_like(acc)
    comm(2)
    for e in range(1, MP):
        arrived(rawr.at[e - 1], r_raw.at[e - 1])
    raw = rawp[rows(mp * 32, 32)] + rawr[0] + rawr[1] + rawr[2]
    norm = jnp.sqrt(jnp.sum(raw * raw, axis=1, keepdims=True) + EPS)
    student = raw / norm
    st32[...] = student
    nm32[...] = jnp.broadcast_to(norm, (32, 128))
    own = rows(256 + q * 32, 32)
    stk[own] = student.astype(BF16)
    for e in range(1, LINE):
        push(stk.at[own], stk.at[own], s_stud.at[e - 1], r_stud.at[e - 1], line_peer(e))
    comm(4)
    theirs = rows((1 - xl) * 128, 128)
    arrived(stk.at[theirs], r_tp.at[0])
    arrived(prow.at[1 - xl], r_tp.at[1])
    for i in range(XL):
        one = jnp.broadcast_to(prow[i][0:1].astype(F32), (128, 128))
        pcol[pl.ds(i * 128, 128)] = one.T
    comm(6)
    for e in range(1, LINE):
        arrived(stk.at[rows(256 + rem(q - e, LINE) * 32, 32)], r_stud.at[e - 1])
    for k in (1, 2):
        complete(k)
        chunk(k)
    far()
    for k in (3, 4, 5, 6, 7, 0):
        complete(k)
        chunk(k)

    lane = lax.broadcasted_iota(jnp.int32, (256, 128), 1)
    cols = jnp.zeros((256, 128), F32)
    for i in range(4):
        cols = jnp.where(lane == i, jnp.sum(acc[i], axis=1, keepdims=True), cols)
    stat[...] = cols.T[0:8]
    for e in range(1, LINE):
        push(stat, statr.at[e - 1], s_stat.at[e - 1], r_stat.at[e - 1], line_peer(e))
    for e in range(1, LINE):
        arrived(statr.at[e - 1], r_stat.at[e - 1])
    sums = stat[...]
    for e in range(1, LINE):
        sums = sums + statr[e - 1]
    zt, zs, lean, pair = (sums[i : i + 1] for i in range(4))
    c_t = jnp.broadcast_to(1.0 / zt, (128, 256)).T
    c_s = jnp.broadcast_to(2.0 / zs, (128, 256)).T

    for k in range(8):
        hit = hits(k)
        coef = jnp.concatenate(
            [
                (
                    ES[k, :, h * 128 : (h + 1) * 128] * c_s
                    - ET[k, :, h * 128 : (h + 1) * 128] * c_t
                    - hit[h].astype(F32)
                ).astype(BF16)
                for h in (0, 1)
            ],
            axis=1,
        )
        more = jnp.dot(coef, captions(k), preferred_element_type=F32)
        if k == 0:
            dp[...] = more
        else:
            dp[...] += more
    dpb[...] = dp[...].astype(BF16)
    for e in (3, 5, 4, 1, 7, 2, 6):
        other = rem(q + e, LINE)
        push(dpb.at[rows(other * 32, 32)], rsr.at[e - 1], s_rs.at[e - 1], r_rs.at[e - 1], line_peer(e))
    part = jnp.sum(lean / zt - jnp.log(zt) + 2.0 * jnp.log(zs) - pair, axis=1, keepdims=True)
    lossy[...] = jnp.broadcast_to(part, (8, 128))
    for e in range(1, Y):
        push(lossy, lossyr.at[e - 1], s_ly.at[e - 1], r_ly.at[e - 1], y_peer(e))
    for e in range(1, Y):
        arrived(lossyr.at[e - 1], r_ly.at[e - 1])
    lossz[...] = lossy[...] + lossyr[0] + lossyr[1] + lossyr[2]
    for e in range(1, Z):
        push(lossz, losszr.at[e - 1], s_lz.at[e - 1], r_lz.at[e - 1], z_peer(e))
    dstud = dp[rows(q * 32, 32)]
    for e in range(1, LINE):
        arrived(rsr.at[e - 1], r_rs.at[e - 1])
        dstud = dstud + rsr[e - 1].astype(F32)
    dstud = dstud * (STUDENT_SCALE / total)
    student = st32[...]
    inner = jnp.sum(student * dstud, axis=1, keepdims=True)
    own = rows(mp * 32, 32)
    drw[own] = ((dstud - student * inner) / nm32[:, 0:1]).astype(BF16)
    for e in (2, 1, 3):
        push(drw.at[own], drw.at[own], s_dr.at[e - 1], r_dr.at[e - 1], mp_peer(e))
    for e in range(1, MP):
        arrived(drw.at[rows(rem(mp - e, MP) * 32, 32)], r_dr.at[e - 1])

    draw = drw[...]
    gs = lax.dot_general(
        hid_v[...], draw, (((0,), (0,)), ((), ())), preferred_element_type=F32
    )
    gsb[...] = gs.astype(BF16)
    group = Y * XL
    for e in range(1, group):
        other = rem(j + e, group)
        push(gsb.at[rows(other * 16, 16)], p1s.at[e - 1], s_p1.at[0, e - 1], r_p1.at[0, e - 1], group_peer(e))
    gs_o[...] = gs
    dpre = (dot_nt(draw, w2_v[...]) * gprime[...]).astype(BF16)
    gf = lax.dot_general(
        clip_v[...], dpre, (((0,), (0,)), ((), ())), preferred_element_type=F32
    )
    gfb[...] = gf.astype(BF16)
    for e in range(1, group):
        other = rem(j + e, group)
        push(gfb.at[rows(other * 96, 96)], p1f.at[e - 1], s_p1.at[1, e - 1], r_p1.at[1, e - 1], group_peer(e))
    gf_o[...] = gf
    one_s = gs_o[rows(j * 16, 16)]
    one_f = gf_o[rows(j * 96, 96)]
    for e in range(1, group):
        arrived(p1s.at[e - 1], r_p1.at[0, e - 1])
        one_s = one_s + p1s[e - 1].astype(F32)
    for e in range(1, group):
        arrived(p1f.at[e - 1], r_p1.at[1, e - 1])
        one_f = one_f + p1f[e - 1].astype(F32)
    own1[pl.ds(0, 96)] = one_f
    for i in range(4):
        own1[pl.ds(96 + 16 * i, 16)] = one_s[:, i * 128 : (i + 1) * 128]
    T[...] = own1[...].astype(BF16)
    for t in range(TILES):

        @pl.when(z != t)
        def _():
            slot = rem(z - t, Z) - 1
            remote(
                T.at[pl.ds(16 * t, 16)], p2r.at[slot], s_p2.at[t], r_p2.at[slot], (y, t, xl, mp)
            ).start()

    loss_sum = lossz[...]
    for e in range(1, Z):
        arrived(losszr.at[e - 1], r_lz.at[e - 1])
        loss_sum = loss_sum + losszr[e - 1]
    loss_o[0, 0] = jnp.sum(loss_sum[0:1, 0:1]) / total

    @pl.when(z < TILES)
    def _():
        tile = rows(z * 16, 16)
        out = own1[tile]
        for e in range(1, Z):
            arrived(p2r.at[e - 1], r_p2.at[e - 1])
            out = out + p2r[e - 1].astype(F32)
        R[tile] = out.astype(BF16)
        for e in range(1, Z):
            remote(R.at[tile], R.at[tile], s_p3.at[e - 1], r_p3.at[z], z_peer(e)).start()

    for t in range(TILES):

        @pl.when(z != t)
        def _():
            arrived(R.at[pl.ds(16 * t, 16)], r_p3.at[t])

    for e in range(1, group):
        push(R, RR.at[e - 1], s_p4.at[e - 1], r_p4.at[e - 1], group_peer(e))

    def write(owner, ref):
        gf_o[rows(owner * 96, 96)] = ref[pl.ds(0, 96)].astype(F32)
        for i in range(4):
            gs_o[rows(owner * 16, 16), i * 128 : (i + 1) * 128] = ref[
                pl.ds(96 + 16 * i, 16)
            ].astype(F32)

    write(j, R)
    for e in range(1, group):
        arrived(RR.at[e - 1], r_p4.at[e - 1])
        write(rem(j - e, group), RR.at[e - 1])

    for copy in sends:
        copy.wait_send()
    for t in range(TILES):

        @pl.when(z != t)
        def _():
            remote(T.at[pl.ds(16 * t, 16)], T.at[pl.ds(16 * t, 16)], s_p2.at[t], s_p2.at[t], me).wait_send()

    @pl.when(z < TILES)
    def _():
        tile = rows(z * 16, 16)
        for e in range(1, Z):
            remote(R.at[tile], R.at[tile], s_p3.at[e - 1], s_p3.at[e - 1], me).wait_send()


def body(clip_feats, teacher_audio, teacher_text, w_first, w_second, pairing):
    vm = pltpu.VMEM
    dma = pltpu.SemaphoreType.DMA
    hbm = pl.BlockSpec(memory_space=pl.ANY)
    scratch = [
        vm((128, 768), BF16), vm((128, 512), BF16), vm((32, 512), BF16),
        vm((768, 128), BF16), vm((128, 512), BF16), vm((1, 128), jnp.int32),
        vm((8, 4, 2, 32, 512), BF16),
        vm((512, 512), BF16), vm((2, 8, 128), jnp.int32), vm((256, 128), F32),
        vm((128, 512), F32), vm((3, 32, 512), F32), vm((32, 512), F32), vm((32, 128), F32),
        vm((128, 128), F32), vm((128, 128), BF16),
        vm((8, 256, 256), F32), vm((8, 256, 256), F32), vm((4, 256, 128), F32),
        vm((8, 256), F32), vm((7, 8, 256), F32),
        vm((256, 512), F32), vm((256, 512), BF16), vm((7, 32, 512), BF16), vm((128, 512), BF16),
        vm((8, 128), F32), vm((3, 8, 128), F32), vm((8, 128), F32), vm((15, 8, 128), F32),
        vm((128, 512), BF16), vm((768, 128), BF16), vm((7, 16, 512), BF16), vm((7, 96, 128), BF16),
        vm((160, 128), F32), vm((160, 128), BF16), vm((15, 16, 128), BF16),
        vm((160, 128), BF16), vm((7, 160, 128), BF16),
        dma((6,)), dma((8, 2)), dma((8, 2)), dma((8, 2)), dma((8, 2)),
        dma((8, 2, 2)), dma((8, 2, 2)),
        dma((3,)), dma((3,)), dma((7,)), dma((7,)), dma((2,)), dma((2,)), dma((7,)), dma((7,)),
        dma((7,)), dma((7,)), dma((3,)), dma((3,)),
        dma((3,)), dma((3,)), dma((15,)), dma((15,)), dma((2, 7)), dma((2, 7)),
        dma((TILES,)), dma((15,)), dma((15,)), dma((TILES,)), dma((7,)), dma((7,)),
    ]
    loss, grad_first, grad_second = pl.pallas_call(
        kernel,
        out_shape=(
            jax.ShapeDtypeStruct((1, 1), F32),
            jax.ShapeDtypeStruct((768, 128), F32),
            jax.ShapeDtypeStruct((128, 512), F32),
        ),
        in_specs=[hbm] * 6,
        out_specs=(
            pl.BlockSpec(memory_space=pltpu.SMEM),
            pl.BlockSpec(memory_space=pltpu.VMEM),
            pl.BlockSpec(memory_space=pltpu.VMEM),
        ),
        scratch_shapes=scratch,
        compiler_params=pltpu.CompilerParams(
            collective_id=0, has_side_effects=True, vmem_limit_bytes=60 * 1024 * 1024
        ),
    )(clip_feats, teacher_audio, teacher_text, w_first, w_second, pairing.reshape(1, 128))
    return loss.reshape(()), grad_first, grad_second


def solution(mesh):
    finer = Mesh(mesh.devices.reshape(Y, Z, XL, MP), ("y", "z", "xl", "mp"))
    return jax.shard_map(
        body,
        mesh=finer,
        in_specs=(
            P(WIDE, None),
            P(WIDE, None),
            P(WIDE + ("mp",), None),
            P(None, "mp"),
            P("mp", None),
            P(WIDE),
        ),
        out_specs=(P(), P(None, "mp"), P("mp", None)),
        check_vma=False,
    )
```

```python
import jax
import jax.numpy as jnp
from jax import lax
from jax.experimental import pallas as pl
from jax.experimental.pallas import tpu as pltpu
from jax.sharding import Mesh
from jax.sharding import PartitionSpec as P

MESH = pl.DeviceIdType.MESH
WIDE = ("y", "z", "xl")
F32 = jnp.float32
BF16 = jnp.bfloat16

Y, Z, XL, MP = 4, 16, 2, 4
LINE = XL * MP
TEACHER_SCALE = 14.0
STUDENT_SCALE = 64.0
EPS = 1e-6
QUAD = 4
GROUP = Y * XL * QUAD


def dot_nt(left, right):
    return lax.dot_general(
        left, right, (((1,), (1,)), ((), ())), preferred_element_type=F32
    )


def normalize(values):
    return values / jnp.sqrt(jnp.sum(values * values, axis=1, keepdims=True) + EPS)


def rows(start, size):
    return pl.ds(pl.multiple_of(start, size), size)


def kernel(
    clip_h, ta_h, tt_h, w1_h, w2_h, pair_h,
    loss_o, gf_o, gs_o,
    clip_v, ta_v, tt_v, w1_v, w2_v, pair_v,
    G, stk, prow, pcol, rawp, rawr, st32, nm32, gprime, hid_t, clip_t,
    ET, ES, cf, acc, stat, statr, dp, dpb, rsr, drw,
    lossy, lossz, W, p1a, p1b, zq, R,
    sem_in, sA, rA, sB, rB, sC, rC,
    s_raw, r_raw, s_stud, r_stud, s_tp, r_tp, s_stat, r_stat, s_rs, r_rs, s_dr, r_dr,
    s_ly, r_ly, s_lz, r_lz, s_p1, r_p1, s_p2, r_p2, s_p3, r_p3,
):
    y, z = lax.axis_index("y"), lax.axis_index("z")
    xl, mp = lax.axis_index("xl"), lax.axis_index("mp")
    q = xl * MP + mp
    zl, zh = lax.rem(z, QUAD), z // QUAD
    o = (y * XL + xl) * QUAD + zl
    total = 128 * Y * Z * XL

    def rem(v, n):
        return lax.rem(v + 4 * n, n)

    def y_peer(e):
        return (rem(y + e, Y), z, xl, mp)

    def z_peer(e):
        return (y, rem(z + e, Z), xl, mp)

    def line_peer(e):
        other = rem(q + e, LINE)
        return (y, z, other // MP, rem(other, MP))

    def mp_peer(e):
        return (y, z, xl, rem(mp + e, MP))

    def group_peer(e):
        other = rem(o + e, GROUP)
        at = (other // (XL * QUAD), zh * QUAD + rem(other, QUAD), rem(other // QUAD, XL), mp)
        return other, at

    def remote(src, dst, send, recv, to):
        return pltpu.make_async_remote_copy(
            src_ref=src, dst_ref=dst, send_sem=send, recv_sem=recv, device_id=to,
            device_id_type=MESH,
        )

    me = (y, z, xl, mp)
    sends = []

    def push(*args):
        copy = remote(*args)
        copy.start()
        sends.append(copy)

    def arrived(dst, recv):
        remote(dst, dst, recv, recv, me).wait_recv()

    ins = [
        pltpu.make_async_copy(h, v, sem_in.at[i])
        for i, (h, v) in enumerate(
            [(tt_h, tt_v), (clip_h, clip_v), (w1_h, w1_v), (w2_h, w2_v), (ta_h, ta_v), (pair_h, pair_v)]
        )
    ]
    for c in ins:
        c.start()
    barrier = pltpu.get_barrier_semaphore()
    partners = [line_peer(e) for e in range(1, LINE)]
    partners += [y_peer(e) for e in range(1, Y)] + [z_peer(e) for e in (1, -1, 2, -2)]
    for p in partners:
        pl.semaphore_signal(barrier, inc=1, device_id=p, device_id_type=MESH)
    ins[0].wait()
    G[0, 0, 0] = normalize(tt_v[...].astype(F32)).astype(BF16)
    pl.semaphore_wait(barrier, len(partners))

    def along_z(o, k, d, send, recv):
        way = 1 - 2 * d
        for step in (2, 1):
            slot, side = k + step, d
            if slot == 8:
                if d != o // 2:
                    continue
                slot, side = 0, 1
            src = G.at[k, o, 0 if k == 0 else d]
            push(src, G.at[slot, o, side], send.at[slot, side], recv.at[slot, side], z_peer(way * step))

    def along_y(k, d):
        for e in (1, 3):
            push(G.at[k, 0, d], G.at[k, Y - e, d], sC.at[k, d, e // 2], rC.at[k, d, e // 2], y_peer(e))

    push(G.at[0, 0, 0], G.at[0, 2, 0], sB.at[0, 0], rB.at[0, 0], y_peer(2))
    for d in (0, 1):
        along_z(0, 0, d, sA, rA)
    along_y(0, 0)

    for c in ins[1:4]:
        c.wait()
    pre = jnp.dot(clip_v[...], w1_v[...], preferred_element_type=F32)
    cdf = 0.5 * (1.0 + lax.erf(pre * 0.7071067811865476))
    hid = (pre * cdf).astype(BF16)
    rawp[...] = jnp.dot(hid, w2_v[...], preferred_element_type=F32)
    for e in (2, 1, 3):
        other = rem(mp + e, MP)
        push(rawp.at[rows(other * 32, 32)], rawr.at[e - 1], s_raw.at[e - 1], r_raw.at[e - 1], mp_peer(e))
    arrived(G.at[0, 2, 0], rB.at[0, 0])
    for d in (0, 1):
        along_z(2, 0, d, sB, rB)
    ins[4].wait()
    ins[5].wait()
    mine = rows(xl * 128, 128)
    stk[mine] = normalize(ta_v[...].astype(F32)).astype(BF16)
    prow[xl] = jnp.broadcast_to(pair_v[...], (8, 128))
    other_x = (y, z, 1 - xl, mp)
    push(stk.at[mine], stk.at[mine], s_tp.at[0], r_tp.at[0], other_x)
    push(prow.at[xl], prow.at[xl], s_tp.at[1], r_tp.at[1], other_x)
    gprime[...] = cdf + pre * (0.3989422804014327 * jnp.exp(-0.5 * pre * pre))
    hid_t[...] = hid.T

    def comm(k):
        for d in (0, 1):
            arrived(G.at[k, 0, d], rA.at[k, d])
            along_z(0, k, d, sA, rA)
        for d in (0, 1):
            arrived(G.at[k, 2, d], rB.at[k, d])
            along_z(2, k, d, sB, rB)
        for d in (0, 1):
            arrived(G.at[k - 1, 0, d], rA.at[k - 1, d])
            along_y(k - 1, d)
            along_y(k, d)

    def far():
        for k, d in ((7, 0), (7, 1), (0, 1)):
            arrived(G.at[k, 0, d], rA.at[k, d])
            along_y(k, d)

    col = lax.broadcasted_iota(jnp.int32, (8, 256), 1)
    way = (col // 32) & 1
    y_at = (y + col // 64) & (Y - 1)
    id_base = ((y_at * Z) * XL + xl) * 128 + mp * 32 + (col & 31)

    def hits(k):
        z_left = rem(z - k, Z)
        z_right = jnp.where(k == 0, rem(z + 8, Z), rem(z + k, Z))
        ids = id_base + jnp.where(way == 1, z_right, z_left) * (XL * 128)
        ids = ids[0:1].astype(F32)
        return [pcol[...] == ids[:, h * 128 : (h + 1) * 128] for h in (0, 1)]

    def captions(k):
        return G[k].reshape(256, 512)

    def chunk(k):
        scores = dot_nt(stk[...], captions(k))
        tlog = TEACHER_SCALE * scores[:256]
        slog = STUDENT_SCALE * scores[256:]
        texp, sexp = jnp.exp(tlog), jnp.exp(slog)
        ET[k] = texp
        ES[k] = sexp
        lean = texp * (tlog - slog)
        hit = hits(k)
        pair = [jnp.where(hit[h], slog[:, h * 128 : (h + 1) * 128], 0.0) for h in (0, 1)]
        acc[0] += texp[:, :128] + texp[:, 128:]
        acc[1] += sexp[:, :128] + sexp[:, 128:]
        acc[2] += lean[:, :128] + lean[:, 128:]
        acc[3] += pair[0] + pair[1]

    def complete(k):
        for d in (0, 1):
            if k == 7 or (k in (1, 3, 5)) or (k == 0 and d == 1):
                arrived(G.at[k, 2, d], rB.at[k, d])
            for e in (1, 3):
                arrived(G.at[k, Y - e, d], rC.at[k, d, e // 2])

    acc[...] = jnp.zeros_like(acc)
    comm(2)
    for e in range(1, MP):
        arrived(rawr.at[e - 1], r_raw.at[e - 1])
    raw = rawp[rows(mp * 32, 32)] + rawr[0] + rawr[1] + rawr[2]
    norm = jnp.sqrt(jnp.sum(raw * raw, axis=1, keepdims=True) + EPS)
    student = raw / norm
    st32[...] = student
    nm32[...] = jnp.broadcast_to(norm, (32, 128))
    own = rows(256 + q * 32, 32)
    stk[own] = student.astype(BF16)
    for e in range(1, LINE):
        push(stk.at[own], stk.at[own], s_stud.at[e - 1], r_stud.at[e - 1], line_peer(e))
    clip_t[...] = clip_v[...].T
    comm(4)
    theirs = rows((1 - xl) * 128, 128)
    arrived(stk.at[theirs], r_tp.at[0])
    arrived(prow.at[1 - xl], r_tp.at[1])
    for i in range(XL):
        one = jnp.broadcast_to(prow[i][0:1].astype(F32), (128, 128))
        pcol[pl.ds(i * 128, 128)] = one.T
    comm(6)
    for e in range(1, LINE):
        arrived(stk.at[rows(256 + rem(q - e, LINE) * 32, 32)], r_stud.at[e - 1])
    for k in (1, 2):
        complete(k)
        chunk(k)
    far()
    for k in (3, 4, 5, 6, 7, 0):
        complete(k)
        chunk(k)

    lane = lax.broadcasted_iota(jnp.int32, (256, 128), 1)
    cols = jnp.zeros((256, 128), F32)
    for i in range(4):
        cols = jnp.where(lane == i, jnp.sum(acc[i], axis=1, keepdims=True), cols)
    stat[...] = cols.T[0:8]
    for e in range(1, LINE):
        push(stat, statr.at[e - 1], s_stat.at[e - 1], r_stat.at[e - 1], line_peer(e))
    for e in range(1, LINE):
        arrived(statr.at[e - 1], r_stat.at[e - 1])
    sums = stat[...]
    for e in range(1, LINE):
        sums = sums + statr[e - 1]
    zt, zs, lean, pair = (sums[i : i + 1] for i in range(4))
    c_t = jnp.broadcast_to(1.0 / zt, (128, 256)).T
    c_s = jnp.broadcast_to(2.0 / zs, (128, 256)).T

    for k in range(8):
        hit = hits(k)
        for h in (0, 1):
            half = pl.ds(h * 128, 128)
            cf[:, k * 256 + h * 128 : k * 256 + (h + 1) * 128] = (
                ES[k, :, half] * c_s - ET[k, :, half] * c_t - hit[h].astype(F32)
            ).astype(BF16)
    dp[...] = jnp.dot(cf[...], G[...].reshape(2048, 512), preferred_element_type=F32)
    dpb[...] = dp[...].astype(BF16)
    for e in (3, 5, 4, 1, 7, 2, 6):
        other = rem(q + e, LINE)
        push(dpb.at[rows(other * 32, 32)], rsr.at[e - 1], s_rs.at[e - 1], r_rs.at[e - 1], line_peer(e))
    part = jnp.sum(lean / zt - jnp.log(zt) + 2.0 * jnp.log(zs) - pair, axis=1, keepdims=True)
    lossy[y] = jnp.broadcast_to(part, (8, 128))
    for e in range(1, Y):
        push(lossy.at[y], lossy.at[y], s_ly.at[e - 1], r_ly.at[e - 1], y_peer(e))
    for e in range(1, Y):
        arrived(lossy.at[rem(y - e, Y)], r_ly.at[e - 1])
    lossz[z] = lossy[0] + lossy[1] + lossy[2] + lossy[3]
    for e in range(1, Z):
        push(lossz.at[z], lossz.at[z], s_lz.at[e - 1], r_lz.at[e - 1], z_peer(e))
    dstud = dp[rows(q * 32, 32)]
    for e in range(1, LINE):
        arrived(rsr.at[e - 1], r_rs.at[e - 1])
        dstud = dstud + rsr[e - 1].astype(F32)
    dstud = dstud * (STUDENT_SCALE / total)
    student = st32[...]
    inner = jnp.sum(student * dstud, axis=1, keepdims=True)
    own = rows(mp * 32, 32)
    drw[own] = ((dstud - student * inner) / nm32[:, 0:1]).astype(BF16)
    for e in (2, 1, 3):
        push(drw.at[own], drw.at[own], s_dr.at[e - 1], r_dr.at[e - 1], mp_peer(e))
    for e in range(1, MP):
        arrived(drw.at[rows(rem(mp - e, MP) * 32, 32)], r_dr.at[e - 1])

    draw = drw[...]
    gs = jnp.dot(hid_t[...], draw, preferred_element_type=F32).astype(BF16)
    for i in range(4):
        W[pl.ds(i * 128, 128)] = gs[:, i * 128 : (i + 1) * 128]

    def scatter(e, other, at):
        return remote(W.at[rows(other * 32, 32)], p1a.at[e - 1], s_p1.at[0, e - 1], r_p1.at[0, e - 1], at)

    def scatter_more(e, other, at):
        return remote(
            W.at[rows(1024 + other * 16, 16)], p1b.at[e - 1], s_p1.at[1, e - 1], r_p1.at[1, e - 1], at
        )

    for e in range(1, GROUP):
        other, at = group_peer(e)

        @pl.when(other < 16)
        def _():
            scatter(e, other, at).start()

    dpre = (dot_nt(draw, w2_v[...]) * gprime[...]).astype(BF16)
    W[pl.ds(512, 768)] = jnp.dot(clip_t[...], dpre, preferred_element_type=F32).astype(BF16)
    for e in range(1, GROUP):
        other, at = group_peer(e)

        @pl.when(other >= 16)
        def _():
            scatter(e, other, at).start()

        @pl.when(other < 16)
        def _():
            scatter_more(e, other, at).start()

    part = W[rows(o * 32, 32)].astype(F32)
    for e in range(1, GROUP):
        arrived(p1a.at[e - 1], r_p1.at[0, e - 1])
        part = part + p1a[e - 1].astype(F32)
    zq[zh, pl.ds(0, 32)] = part.astype(BF16)
    zq[zh, pl.ds(32, 16)] = jnp.zeros((16, 128), BF16)

    @pl.when(o < 16)
    def _():
        more = W[rows(1024 + o * 16, 16)].astype(F32)
        for e in range(1, GROUP):
            arrived(p1b.at[e - 1], r_p1.at[1, e - 1])
            more = more + p1b[e - 1].astype(F32)
        zq[zh, pl.ds(32, 16)] = more.astype(BF16)

    for e in range(1, QUAD):
        push(zq.at[zh], zq.at[zh], s_p2.at[e - 1], r_p2.at[e - 1], z_peer(QUAD * e))
    for e in range(1, Z):
        arrived(lossz.at[rem(z - e, Z)], r_lz.at[e - 1])
    loss_sum = lossz[0]
    for i in range(1, Z):
        loss_sum = loss_sum + lossz[i]
    loss_o[0, 0] = jnp.sum(loss_sum[0:1, 0:1]) / total
    for e in range(1, QUAD):
        arrived(zq.at[rem(zh - e, QUAD)], r_p2.at[e - 1])
    whole = zq[0].astype(F32)
    for i in range(1, QUAD):
        whole = whole + zq[i].astype(F32)
    whole = whole.astype(BF16)
    first, second = rows(o * 32, 32), rows(1024 + o * 16, 16)
    R[first] = whole[:32]
    for e in range(1, GROUP):
        push(R.at[first], R.at[first], s_p3.at[0, e - 1], r_p3.at[0, e - 1], group_peer(e)[1])

    @pl.when(o < 16)
    def _():
        R[second] = whole[32:]
        for e in range(1, GROUP):
            remote(R.at[second], R.at[second], s_p3.at[1, e - 1], r_p3.at[1, e - 1], group_peer(e)[1]).start()

    for e in range(1, GROUP):
        other = rem(o - e, GROUP)
        arrived(R.at[rows(other * 32, 32)], r_p3.at[0, e - 1])

        @pl.when(other < 16)
        def _():
            arrived(R.at[rows(1024 + other * 16, 16)], r_p3.at[1, e - 1])

    for i in range(4):
        gs_o[:, i * 128 : (i + 1) * 128] = R[pl.ds(i * 128, 128)].astype(F32)
    gf_o[...] = R[pl.ds(512, 768)].astype(F32)

    for copy in sends:
        copy.wait_send()
    for e in range(1, GROUP):
        other, at = group_peer(e)
        scatter(e, other, at).wait_send()

        @pl.when(other < 16)
        def _():
            scatter_more(e, other, at).wait_send()

    @pl.when(o < 16)
    def _():
        for e in range(1, GROUP):
            remote(R.at[second], R.at[second], s_p3.at[1, e - 1], r_p3.at[1, e - 1], me).wait_send()


def body(clip_feats, teacher_audio, teacher_text, w_first, w_second, pairing):
    vm = pltpu.VMEM
    dma = pltpu.SemaphoreType.DMA
    hbm = pl.BlockSpec(memory_space=pl.ANY)
    scratch = [
        vm((128, 768), BF16), vm((128, 512), BF16), vm((32, 512), BF16),
        vm((768, 128), BF16), vm((128, 512), BF16), vm((1, 128), jnp.int32),
        vm((8, 4, 2, 32, 512), BF16),
        vm((512, 512), BF16), vm((2, 8, 128), jnp.int32), vm((256, 128), F32),
        vm((128, 512), F32), vm((3, 32, 512), F32), vm((32, 512), F32), vm((32, 128), F32),
        vm((128, 128), F32), vm((128, 128), BF16), vm((768, 128), BF16),
        vm((8, 256, 256), F32), vm((8, 256, 256), F32), vm((256, 2048), BF16), vm((4, 256, 128), F32),
        vm((8, 256), F32), vm((7, 8, 256), F32),
        vm((256, 512), F32), vm((256, 512), BF16), vm((7, 32, 512), BF16), vm((128, 512), BF16),
        vm((Y, 8, 128), F32), vm((Z, 8, 128), F32), vm((1280, 128), BF16),
        vm((GROUP - 1, 32, 128), BF16), vm((GROUP - 1, 16, 128), BF16), vm((QUAD, 48, 128), BF16),
        vm((1280, 128), BF16),
        dma((6,)), dma((8, 2)), dma((8, 2)), dma((8, 2)), dma((8, 2)),
        dma((8, 2, 2)), dma((8, 2, 2)),
        dma((3,)), dma((3,)), dma((7,)), dma((7,)), dma((2,)), dma((2,)), dma((7,)), dma((7,)),
        dma((7,)), dma((7,)), dma((3,)), dma((3,)),
        dma((3,)), dma((3,)), dma((15,)), dma((15,)), dma((2, GROUP - 1)), dma((2, GROUP - 1)),
        dma((QUAD - 1,)), dma((QUAD - 1,)), dma((2, GROUP - 1)), dma((2, GROUP - 1)),
    ]
    loss, grad_first, grad_second = pl.pallas_call(
        kernel,
        out_shape=(
            jax.ShapeDtypeStruct((1, 1), F32),
            jax.ShapeDtypeStruct((768, 128), F32),
            jax.ShapeDtypeStruct((128, 512), F32),
        ),
        in_specs=[hbm] * 6,
        out_specs=(
            pl.BlockSpec(memory_space=pltpu.SMEM),
            pl.BlockSpec(memory_space=pltpu.VMEM),
            pl.BlockSpec(memory_space=pltpu.VMEM),
        ),
        scratch_shapes=scratch,
        compiler_params=pltpu.CompilerParams(
            collective_id=0, has_side_effects=True, vmem_limit_bytes=60 * 1024 * 1024
        ),
    )(clip_feats, teacher_audio, teacher_text, w_first, w_second, pairing.reshape(1, 128))
    return loss.reshape(()), grad_first, grad_second


def solution(mesh):
    finer = Mesh(mesh.devices.reshape(Y, Z, XL, MP), ("y", "z", "xl", "mp"))
    return jax.shard_map(
        body,
        mesh=finer,
        in_specs=(
            P(WIDE, None),
            P(WIDE, None),
            P(WIDE + ("mp",), None),
            P(None, "mp"),
            P("mp", None),
            P(WIDE),
        ),
        out_specs=(P(), P(None, "mp"), P("mp", None)),
        check_vma=False,
    )
```

```python
import jax
import jax.numpy as jnp
from jax import lax
from jax.experimental import pallas as pl
from jax.experimental.pallas import tpu as pltpu
from jax.sharding import Mesh
from jax.sharding import PartitionSpec as P

MESH = pl.DeviceIdType.MESH
WIDE = ("y", "z", "xl")
F32 = jnp.float32
BF16 = jnp.bfloat16

Y, Z, XL, MP = 4, 16, 2, 4
LINE = XL * MP
TEACHER_SCALE = 14.0
STUDENT_SCALE = 64.0
EPS = 1e-6
GROUP = Y * XL
SLICE = 160
TILES = 10


def dot_nt(left, right):
    return lax.dot_general(
        left, right, (((1,), (1,)), ((), ())), preferred_element_type=F32
    )


def normalize(values):
    return values / jnp.sqrt(jnp.sum(values * values, axis=1, keepdims=True) + EPS)


def rows(start, size):
    return pl.ds(pl.multiple_of(start, size), size)


def kernel(
    clip_h, ta_h, tt_h, w1_h, w2_h, pair_h,
    loss_o, gf_h, gs_h,
    clip_v, ta_v, tt_v, w1_v, w2_v, pair_v,
    G, stk, prow, pcol, rawp, rawr, st32, nm32, gprime, hid_t, clip_t,
    ET, ES, cf, acc, stat, statr, dp, dpb, rsr, drw,
    lossy, lossz, W, p1, own1, T, p2r, R, Rs,
    sem_in, sA, rA, sB, rB, sC, rC,
    s_raw, r_raw, s_stud, r_stud, s_tp, r_tp, s_stat, r_stat, s_rs, r_rs, s_dr, r_dr,
    s_ly, r_ly, s_lz, r_lz, s_p1, r_p1, s_p2, r_p2, s_p3, r_p3, s_p4, r_p4,
):
    y, z = lax.axis_index("y"), lax.axis_index("z")
    xl, mp = lax.axis_index("xl"), lax.axis_index("mp")
    q = xl * MP + mp
    j = y * XL + xl
    total = 128 * Y * Z * XL

    def rem(v, n):
        return lax.rem(v + 4 * n, n)

    def y_peer(e):
        return (rem(y + e, Y), z, xl, mp)

    def z_peer(e):
        return (y, rem(z + e, Z), xl, mp)

    def line_peer(e):
        other = rem(q + e, LINE)
        return (y, z, other // MP, rem(other, MP))

    def mp_peer(e):
        return (y, z, xl, rem(mp + e, MP))

    def group_peer(e):
        other = rem(j + e, GROUP)
        return other, (other // XL, z, rem(other, XL), mp)

    def remote(src, dst, send, recv, to):
        return pltpu.make_async_remote_copy(
            src_ref=src, dst_ref=dst, send_sem=send, recv_sem=recv, device_id=to,
            device_id_type=MESH,
        )

    me = (y, z, xl, mp)
    sends = []

    def push(*args):
        copy = remote(*args)
        copy.start()
        sends.append(copy)

    def arrived(dst, recv):
        remote(dst, dst, recv, recv, me).wait_recv()

    ins = [
        pltpu.make_async_copy(h, v, sem_in.at[i])
        for i, (h, v) in enumerate(
            [(tt_h, tt_v), (clip_h, clip_v), (w1_h, w1_v), (w2_h, w2_v), (ta_h, ta_v), (pair_h, pair_v)]
        )
    ]
    for c in ins:
        c.start()
    barrier = pltpu.get_barrier_semaphore()
    partners = [line_peer(e) for e in range(1, LINE)]
    partners += [y_peer(e) for e in range(1, Y)] + [z_peer(e) for e in (1, -1, 2, -2)]
    for p in partners:
        pl.semaphore_signal(barrier, inc=1, device_id=p, device_id_type=MESH)
    ins[0].wait()
    G[0, 0, 0] = normalize(tt_v[...].astype(F32)).astype(BF16)
    pl.semaphore_wait(barrier, len(partners))

    def along_z(o, k, d, send, recv):
        way = 1 - 2 * d
        for step in (2, 1):
            slot, side = k + step, d
            if slot == 8:
                if d != o // 2:
                    continue
                slot, side = 0, 1
            src = G.at[k, o, 0 if k == 0 else d]
            push(src, G.at[slot, o, side], send.at[slot, side], recv.at[slot, side], z_peer(way * step))

    def along_y(k, d):
        for e in (1, 3):
            push(G.at[k, 0, d], G.at[k, Y - e, d], sC.at[k, d, e // 2], rC.at[k, d, e // 2], y_peer(e))

    push(G.at[0, 0, 0], G.at[0, 2, 0], sB.at[0, 0], rB.at[0, 0], y_peer(2))
    for d in (0, 1):
        along_z(0, 0, d, sA, rA)
    along_y(0, 0)

    for c in ins[1:4]:
        c.wait()
    pre = jnp.dot(clip_v[...], w1_v[...], preferred_element_type=F32)
    cdf = 0.5 * (1.0 + lax.erf(pre * 0.7071067811865476))
    hid = (pre * cdf).astype(BF16)
    rawp[...] = jnp.dot(hid, w2_v[...], preferred_element_type=F32)
    for e in (2, 1, 3):
        other = rem(mp + e, MP)
        push(rawp.at[rows(other * 32, 32)], rawr.at[e - 1], s_raw.at[e - 1], r_raw.at[e - 1], mp_peer(e))
    arrived(G.at[0, 2, 0], rB.at[0, 0])
    for d in (0, 1):
        along_z(2, 0, d, sB, rB)
    ins[4].wait()
    ins[5].wait()
    mine = rows(xl * 128, 128)
    stk[mine] = normalize(ta_v[...].astype(F32)).astype(BF16)
    prow[xl] = jnp.broadcast_to(pair_v[...], (8, 128))
    other_x = (y, z, 1 - xl, mp)
    push(stk.at[mine], stk.at[mine], s_tp.at[0], r_tp.at[0], other_x)
    push(prow.at[xl], prow.at[xl], s_tp.at[1], r_tp.at[1], other_x)
    gprime[...] = cdf + pre * (0.3989422804014327 * jnp.exp(-0.5 * pre * pre))
    hid_t[...] = hid.T

    def comm(k):
        for d in (0, 1):
            arrived(G.at[k, 0, d], rA.at[k, d])
            along_z(0, k, d, sA, rA)
        for d in (0, 1):
            arrived(G.at[k, 2, d], rB.at[k, d])
            along_z(2, k, d, sB, rB)
        for d in (0, 1):
            arrived(G.at[k - 1, 0, d], rA.at[k - 1, d])
            along_y(k - 1, d)
            along_y(k, d)

    def far():
        for k, d in ((7, 0), (7, 1), (0, 1)):
            arrived(G.at[k, 0, d], rA.at[k, d])
            along_y(k, d)

    col = lax.broadcasted_iota(jnp.int32, (8, 256), 1)
    way = (col // 32) & 1
    y_at = (y + col // 64) & (Y - 1)
    id_base = ((y_at * Z) * XL + xl) * 128 + mp * 32 + (col & 31)

    def hits(k):
        z_left = rem(z - k, Z)
        z_right = jnp.where(k == 0, rem(z + 8, Z), rem(z + k, Z))
        ids = id_base + jnp.where(way == 1, z_right, z_left) * (XL * 128)
        ids = ids[0:1].astype(F32)
        return [pcol[...] == ids[:, h * 128 : (h + 1) * 128] for h in (0, 1)]

    def captions(k):
        return G[k].reshape(256, 512)

    def chunk(k):
        scores = dot_nt(stk[...], captions(k))
        tlog = TEACHER_SCALE * scores[:256]
        slog = STUDENT_SCALE * scores[256:]
        texp, sexp = jnp.exp(tlog), jnp.exp(slog)
        ET[k] = texp
        ES[k] = sexp
        lean = texp * (tlog - slog)
        hit = hits(k)
        pair = [jnp.where(hit[h], slog[:, h * 128 : (h + 1) * 128], 0.0) for h in (0, 1)]
        acc[0] += texp[:, :128] + texp[:, 128:]
        acc[1] += sexp[:, :128] + sexp[:, 128:]
        acc[2] += lean[:, :128] + lean[:, 128:]
        acc[3] += pair[0] + pair[1]

    def complete(k):
        for d in (0, 1):
            if k == 7 or (k in (1, 3, 5)) or (k == 0 and d == 1):
                arrived(G.at[k, 2, d], rB.at[k, d])
            for e in (1, 3):
                arrived(G.at[k, Y - e, d], rC.at[k, d, e // 2])

    acc[...] = jnp.zeros_like(acc)
    comm(2)
    for e in range(1, MP):
        arrived(rawr.at[e - 1], r_raw.at[e - 1])
    raw = rawp[rows(mp * 32, 32)] + rawr[0] + rawr[1] + rawr[2]
    norm = jnp.sqrt(jnp.sum(raw * raw, axis=1, keepdims=True) + EPS)
    student = raw / norm
    st32[...] = student
    nm32[...] = jnp.broadcast_to(norm, (32, 128))
    own = rows(256 + q * 32, 32)
    stk[own] = student.astype(BF16)
    for e in range(1, LINE):
        push(stk.at[own], stk.at[own], s_stud.at[e - 1], r_stud.at[e - 1], line_peer(e))
    comm(4)
    theirs = rows((1 - xl) * 128, 128)
    arrived(stk.at[theirs], r_tp.at[0])
    arrived(prow.at[1 - xl], r_tp.at[1])
    for i in range(XL):
        one = jnp.broadcast_to(prow[i][0:1].astype(F32), (128, 128))
        pcol[pl.ds(i * 128, 128)] = one.T
    comm(6)
    for e in range(1, LINE):
        arrived(stk.at[rows(256 + rem(q - e, LINE) * 32, 32)], r_stud.at[e - 1])
    for k in (1, 2):
        complete(k)
        chunk(k)
    far()
    for k in (3, 4, 5, 6, 7, 0):
        complete(k)
        chunk(k)
        if k == 3:
            clip_t[...] = clip_v[...].T

    lane = lax.broadcasted_iota(jnp.int32, (256, 128), 1)
    cols = jnp.zeros((256, 128), F32)
    for i in range(4):
        cols = jnp.where(lane == i, jnp.sum(acc[i], axis=1, keepdims=True), cols)
    stat[...] = cols.T[0:8]
    for e in range(1, LINE):
        push(stat, statr.at[e - 1], s_stat.at[e - 1], r_stat.at[e - 1], line_peer(e))
    for e in range(1, LINE):
        arrived(statr.at[e - 1], r_stat.at[e - 1])
    sums = stat[...]
    for e in range(1, LINE):
        sums = sums + statr[e - 1]
    zt, zs, lean, pair = (sums[i : i + 1] for i in range(4))
    c_t = jnp.broadcast_to(1.0 / zt, (128, 256)).T
    c_s = jnp.broadcast_to(2.0 / zs, (128, 256)).T

    for k in range(8):
        hit = hits(k)
        for h in (0, 1):
            half = pl.ds(h * 128, 128)
            cf[:, k * 256 + h * 128 : k * 256 + (h + 1) * 128] = (
                ES[k, :, half] * c_s - ET[k, :, half] * c_t - hit[h].astype(F32)
            ).astype(BF16)
    dp[...] = jnp.dot(cf[...], G[...].reshape(2048, 512), preferred_element_type=F32)
    dpb[...] = dp[...].astype(BF16)
    for e in (3, 5, 4, 1, 7, 2, 6):
        other = rem(q + e, LINE)
        push(dpb.at[rows(other * 32, 32)], rsr.at[e - 1], s_rs.at[e - 1], r_rs.at[e - 1], line_peer(e))
    part = jnp.sum(lean / zt - jnp.log(zt) + 2.0 * jnp.log(zs) - pair, axis=1, keepdims=True)
    lossy[y] = jnp.broadcast_to(part, (8, 128))
    for e in range(1, Y):
        push(lossy.at[y], lossy.at[y], s_ly.at[e - 1], r_ly.at[e - 1], y_peer(e))
    for e in range(1, Y):
        arrived(lossy.at[rem(y - e, Y)], r_ly.at[e - 1])
    lossz[z] = lossy[0] + lossy[1] + lossy[2] + lossy[3]
    for e in range(1, Z):
        push(lossz.at[z], lossz.at[z], s_lz.at[e - 1], r_lz.at[e - 1], z_peer(e))
    dstud = dp[rows(q * 32, 32)]
    for e in range(1, LINE):
        arrived(rsr.at[e - 1], r_rs.at[e - 1])
        dstud = dstud + rsr[e - 1].astype(F32)
    dstud = dstud * (STUDENT_SCALE / total)
    student = st32[...]
    inner = jnp.sum(student * dstud, axis=1, keepdims=True)
    own = rows(mp * 32, 32)
    drw[own] = ((dstud - student * inner) / nm32[:, 0:1]).astype(BF16)
    for e in (2, 1, 3):
        push(drw.at[own], drw.at[own], s_dr.at[e - 1], r_dr.at[e - 1], mp_peer(e))
    for e in range(1, MP):
        arrived(drw.at[rows(rem(mp - e, MP) * 32, 32)], r_dr.at[e - 1])

    draw = drw[...]
    gs = jnp.dot(hid_t[...], draw, preferred_element_type=F32).astype(BF16)
    for jj in range(GROUP):
        for i in range(4):
            W[pl.ds(jj * SLICE + 96 + i * 16, 16)] = gs[jj * 16 : (jj + 1) * 16, i * 128 : (i + 1) * 128]

    def scatter(part, start, size):
        for e in range(1, GROUP):
            other, at = group_peer(e)
            src = W.at[pl.ds(pl.multiple_of(other * SLICE + start, 32), size)]
            push(src, p1.at[e - 1, pl.ds(start, size)], s_p1.at[part, e - 1], r_p1.at[part, e - 1], at)

    scatter(0, 96, 64)
    dpre = (dot_nt(draw, w2_v[...]) * gprime[...]).astype(BF16)
    gf = jnp.dot(clip_t[...], dpre, preferred_element_type=F32).astype(BF16)
    for jj in range(GROUP):
        W[pl.ds(jj * SLICE, 96)] = gf[jj * 96 : (jj + 1) * 96]
    scatter(1, 0, 96)
    part = W[rows(j * SLICE, SLICE)].astype(F32)
    for e in range(1, GROUP):
        arrived(p1.at[e - 1, pl.ds(96, 64)], r_p1.at[0, e - 1])
        arrived(p1.at[e - 1, pl.ds(0, 96)], r_p1.at[1, e - 1])
        part = part + p1[e - 1].astype(F32)
    own1[...] = part
    T[...] = part.astype(BF16)

    def to_owner(t):
        owner = 8 * t // 5
        slot = rem(z - owner, Z) - 1
        tile = T.at[pl.ds(16 * t, 16)]
        return remote(tile, p2r.at[slot], s_p2.at[t], r_p2.at[slot], (y, owner, xl, mp))

    for t in range(TILES):

        @pl.when(z != 8 * t // 5)
        def _():
            to_owner(t).start()

    my_tile = lax.min((5 * z + 7) // 8, TILES - 1)
    owns = 8 * my_tile // 5 == z
    tile = rows(my_tile * 16, 16)

    @pl.when(owns)
    def _():
        out = own1[tile]
        for e in range(1, Z):
            arrived(p2r.at[e - 1], r_p2.at[e - 1])
            out = out + p2r[e - 1].astype(F32)
        R[tile] = out.astype(BF16)
        for e in range(1, Z):
            remote(R.at[tile], R.at[tile], s_p3.at[e - 1], r_p3.at[my_tile], z_peer(e)).start()

    for e in range(1, Z):
        arrived(lossz.at[rem(z - e, Z)], r_lz.at[e - 1])
    loss_sum = lossz[0]
    for i in range(1, Z):
        loss_sum = loss_sum + lossz[i]
    loss_o[0, 0] = jnp.sum(loss_sum[0:1, 0:1]) / total

    for t in range(TILES):

        @pl.when(z != 8 * t // 5)
        def _():
            arrived(R.at[pl.ds(16 * t, 16)], r_p3.at[t])

    Rs[...] = jnp.concatenate([R[pl.ds(96 + i * 16, 16)] for i in range(4)], axis=1)
    mine = [(R.at[pl.ds(0, 96)], gf_h.at[rows(j * 96, 96)]), (Rs, gs_h.at[rows(j * 16, 16)])]
    keep = []
    for i, (src, dst) in enumerate(mine):
        for e in range(1, GROUP):
            push(src, dst, s_p4.at[i, e - 1], r_p4.at[i, e - 1], group_peer(e)[1])
        keep.append(pltpu.make_async_copy(src, dst, sem_in.at[6 + i]))
        keep[-1].start()
    for copy in sends:
        copy.wait_send()
    for t in range(TILES):

        @pl.when(z != 8 * t // 5)
        def _():
            to_owner(t).wait_send()

    @pl.when(owns)
    def _():
        for e in range(1, Z):
            remote(R.at[tile], R.at[tile], s_p3.at[e - 1], s_p3.at[e - 1], me).wait_send()

    for copy in keep:
        copy.wait()
    for e in range(1, GROUP):
        other = rem(j - e, GROUP)
        arrived(gf_h.at[rows(other * 96, 96)], r_p4.at[0, e - 1])
        arrived(gs_h.at[rows(other * 16, 16)], r_p4.at[1, e - 1])


def body(clip_feats, teacher_audio, teacher_text, w_first, w_second, pairing):
    vm = pltpu.VMEM
    dma = pltpu.SemaphoreType.DMA
    hbm = pl.BlockSpec(memory_space=pl.ANY)
    scratch = [
        vm((128, 768), BF16), vm((128, 512), BF16), vm((32, 512), BF16),
        vm((768, 128), BF16), vm((128, 512), BF16), vm((1, 128), jnp.int32),
        vm((8, 4, 2, 32, 512), BF16),
        vm((512, 512), BF16), vm((2, 8, 128), jnp.int32), vm((256, 128), F32),
        vm((128, 512), F32), vm((3, 32, 512), F32), vm((32, 512), F32), vm((32, 128), F32),
        vm((128, 128), F32), vm((128, 128), BF16), vm((768, 128), BF16),
        vm((8, 256, 256), F32), vm((8, 256, 256), F32), vm((256, 2048), BF16), vm((4, 256, 128), F32),
        vm((8, 256), F32), vm((7, 8, 256), F32),
        vm((256, 512), F32), vm((256, 512), BF16), vm((7, 32, 512), BF16), vm((128, 512), BF16),
        vm((Y, 8, 128), F32), vm((Z, 8, 128), F32), vm((1280, 128), BF16),
        vm((GROUP - 1, SLICE, 128), BF16), vm((SLICE, 128), F32), vm((SLICE, 128), BF16),
        vm((Z - 1, 16, 128), BF16), vm((SLICE, 128), BF16), vm((16, 512), BF16),
        dma((8,)), dma((8, 2)), dma((8, 2)), dma((8, 2)), dma((8, 2)),
        dma((8, 2, 2)), dma((8, 2, 2)),
        dma((3,)), dma((3,)), dma((7,)), dma((7,)), dma((2,)), dma((2,)), dma((7,)), dma((7,)),
        dma((7,)), dma((7,)), dma((3,)), dma((3,)),
        dma((3,)), dma((3,)), dma((15,)), dma((15,)), dma((2, GROUP - 1)), dma((2, GROUP - 1)),
        dma((TILES,)), dma((Z - 1,)), dma((Z - 1,)), dma((TILES,)), dma((2, GROUP - 1)), dma((2, GROUP - 1)),
    ]
    loss, grad_first, grad_second = pl.pallas_call(
        kernel,
        out_shape=(
            jax.ShapeDtypeStruct((1, 1), F32),
            jax.ShapeDtypeStruct((768, 128), BF16),
            jax.ShapeDtypeStruct((128, 512), BF16),
        ),
        in_specs=[hbm] * 6,
        out_specs=(pl.BlockSpec(memory_space=pltpu.SMEM), hbm, hbm),
        scratch_shapes=scratch,
        compiler_params=pltpu.CompilerParams(
            collective_id=0, has_side_effects=True, vmem_limit_bytes=60 * 1024 * 1024
        ),
    )(clip_feats, teacher_audio, teacher_text, w_first, w_second, pairing.reshape(1, 128))
    return loss.reshape(()), grad_first.astype(F32), grad_second.astype(F32)


def solution(mesh):
    finer = Mesh(mesh.devices.reshape(Y, Z, XL, MP), ("y", "z", "xl", "mp"))
    return jax.shard_map(
        body,
        mesh=finer,
        in_specs=(
            P(WIDE, None),
            P(WIDE, None),
            P(WIDE + ("mp",), None),
            P(None, "mp"),
            P("mp", None),
            P(WIDE),
        ),
        out_specs=(P(), P(None, "mp"), P("mp", None)),
        check_vma=False,
    )
```

```python
import jax
import jax.numpy as jnp
from jax import lax
from jax.experimental import pallas as pl
from jax.experimental.pallas import tpu as pltpu
from jax.sharding import Mesh
from jax.sharding import PartitionSpec as P

MESH = pl.DeviceIdType.MESH
WIDE = ("y", "z", "xl")
F32 = jnp.float32
BF16 = jnp.bfloat16

Y, Z, XL, MP = 4, 16, 2, 4
LINE = XL * MP
TEACHER_SCALE = 14.0
STUDENT_SCALE = 64.0
EPS = 1e-6
GROUP = Y * XL
SLICE = 160
TILES = 10


def dot_nt(left, right):
    return lax.dot_general(
        left, right, (((1,), (1,)), ((), ())), preferred_element_type=F32
    )


def normalize(values):
    return values / jnp.sqrt(jnp.sum(values * values, axis=1, keepdims=True) + EPS)


def rows(start, size):
    return pl.ds(pl.multiple_of(start, size), size)


def kernel(
    clip_h, ta_h, tt_h, w1_h, w2_h, pair_h,
    loss_o, gf_h, gs_h,
    clip_v, ta_v, tt_v, w1_v, w2_v, pair_v,
    G, stk, prow, pcol, rawp, rawr, st32, nm32, gprime, hid_t, clip_t,
    ET, ES, cf, acc, stat, statr, dp, dpb, rsr, drw,
    lossy, lossz, W, p1, own1, T, p2r, R, Rs,
    sem_in, sA, rA, sB, rB, sC, rC,
    s_raw, r_raw, s_stud, r_stud, s_tp, r_tp, s_stat, r_stat, s_rs, r_rs, s_dr, r_dr,
    s_ly, r_ly, s_lz, r_lz, s_p1, r_p1, s_p2, r_p2, s_p3, r_p3, s_p4, r_p4,
):
    y, z = lax.axis_index("y"), lax.axis_index("z")
    xl, mp = lax.axis_index("xl"), lax.axis_index("mp")
    q = xl * MP + mp
    j = y * XL + xl
    total = 128 * Y * Z * XL

    def rem(v, n):
        return lax.rem(v + 4 * n, n)

    def y_peer(e):
        return (rem(y + e, Y), z, xl, mp)

    def z_peer(e):
        return (y, rem(z + e, Z), xl, mp)

    def line_peer(e):
        other = rem(q + e, LINE)
        return (y, z, other // MP, rem(other, MP))

    def mp_peer(e):
        return (y, z, xl, rem(mp + e, MP))

    def group_peer(e):
        other = rem(j + e, GROUP)
        return other, (other // XL, z, rem(other, XL), mp)

    def remote(src, dst, send, recv, to):
        return pltpu.make_async_remote_copy(
            src_ref=src, dst_ref=dst, send_sem=send, recv_sem=recv, device_id=to,
            device_id_type=MESH,
        )

    me = (y, z, xl, mp)
    sends = []

    def push(*args):
        copy = remote(*args)
        copy.start()
        sends.append(copy)

    def arrived(dst, recv):
        remote(dst, dst, recv, recv, me).wait_recv()

    ins = [
        pltpu.make_async_copy(h, v, sem_in.at[i])
        for i, (h, v) in enumerate(
            [(tt_h, tt_v), (clip_h, clip_v), (w1_h, w1_v), (w2_h, w2_v), (ta_h, ta_v), (pair_h, pair_v)]
        )
    ]
    for c in ins:
        c.start()
    barrier = pltpu.get_barrier_semaphore()
    partners = [line_peer(e) for e in range(1, LINE)]
    partners += [y_peer(e) for e in range(1, Y)] + [z_peer(e) for e in (1, -1, 2, -2)]
    for p in partners:
        pl.semaphore_signal(barrier, inc=1, device_id=p, device_id_type=MESH)
    ins[0].wait()
    G[0, 0, 0] = normalize(tt_v[...].astype(F32)).astype(BF16)
    pl.semaphore_wait(barrier, len(partners))

    def along_z(o, k, d, send, recv):
        way = 1 - 2 * d
        for step in (2, 1):
            slot, side = k + step, d
            if slot == 8:
                if d != o // 2:
                    continue
                slot, side = 0, 1
            src = G.at[k, o, 0 if k == 0 else d]
            push(src, G.at[slot, o, side], send.at[slot, side], recv.at[slot, side], z_peer(way * step))

    def along_y(k, d):
        for e in (1, 3):
            push(G.at[k, 0, d], G.at[k, Y - e, d], sC.at[k, d, e // 2], rC.at[k, d, e // 2], y_peer(e))

    push(G.at[0, 0, 0], G.at[0, 2, 0], sB.at[0, 0], rB.at[0, 0], y_peer(2))
    for d in (0, 1):
        along_z(0, 0, d, sA, rA)
    along_y(0, 0)

    for c in ins[1:4]:
        c.wait()
    pre = jnp.dot(clip_v[...], w1_v[...], preferred_element_type=F32)
    cdf = 0.5 * (1.0 + lax.erf(pre * 0.7071067811865476))
    hid = (pre * cdf).astype(BF16)
    rawp[...] = jnp.dot(hid, w2_v[...], preferred_element_type=F32)
    for e in (2, 1, 3):
        other = rem(mp + e, MP)
        push(rawp.at[rows(other * 32, 32)], rawr.at[e - 1], s_raw.at[e - 1], r_raw.at[e - 1], mp_peer(e))
    arrived(G.at[0, 2, 0], rB.at[0, 0])
    for d in (0, 1):
        along_z(2, 0, d, sB, rB)
    ins[4].wait()
    ins[5].wait()
    mine = rows(xl * 128, 128)
    stk[mine] = normalize(ta_v[...].astype(F32)).astype(BF16)
    prow[xl] = jnp.broadcast_to(pair_v[...], (8, 128))
    other_x = (y, z, 1 - xl, mp)
    push(stk.at[mine], stk.at[mine], s_tp.at[0], r_tp.at[0], other_x)
    push(prow.at[xl], prow.at[xl], s_tp.at[1], r_tp.at[1], other_x)
    gprime[...] = cdf + pre * (0.3989422804014327 * jnp.exp(-0.5 * pre * pre))
    hid_t[...] = hid.T

    def own_block(k):
        for d in (0, 1):
            arrived(G.at[k, 0, d], rA.at[k, d])
            along_z(0, k, d, sA, rA)
        for d in (0, 1):
            along_y(k, d)
        for d in (0, 1):
            arrived(G.at[k - 1, 0, d], rA.at[k - 1, d])
            along_y(k - 1, d)

    def far_block(k):
        for d in (0, 1):
            arrived(G.at[k, 2, d], rB.at[k, d])
            along_z(2, k, d, sB, rB)

    def far():
        for k, d in ((7, 0), (7, 1), (0, 1)):
            arrived(G.at[k, 0, d], rA.at[k, d])
            along_y(k, d)

    col = lax.broadcasted_iota(jnp.int32, (8, 256), 1)
    way = (col // 32) & 1
    y_at = (y + col // 64) & (Y - 1)
    id_base = ((y_at * Z) * XL + xl) * 128 + mp * 32 + (col & 31)

    def hits(k):
        z_left = rem(z - k, Z)
        z_right = jnp.where(k == 0, rem(z + 8, Z), rem(z + k, Z))
        ids = id_base + jnp.where(way == 1, z_right, z_left) * (XL * 128)
        ids = ids[0:1].astype(F32)
        return [pcol[...] == ids[:, h * 128 : (h + 1) * 128] for h in (0, 1)]

    def captions(k):
        return G[k].reshape(256, 512)

    def chunk(k):
        scores = dot_nt(stk[...], captions(k))
        tlog = TEACHER_SCALE * scores[:256]
        slog = STUDENT_SCALE * scores[256:]
        texp, sexp = jnp.exp(tlog), jnp.exp(slog)
        ET[k] = texp
        ES[k] = sexp
        lean = texp * (tlog - slog)
        hit = hits(k)
        pair = [jnp.where(hit[h], slog[:, h * 128 : (h + 1) * 128], 0.0) for h in (0, 1)]
        acc[0] += texp[:, :128] + texp[:, 128:]
        acc[1] += sexp[:, :128] + sexp[:, 128:]
        acc[2] += lean[:, :128] + lean[:, 128:]
        acc[3] += pair[0] + pair[1]

    def complete(k):
        for d in (0, 1):
            if k == 7 or (k in (1, 3, 5)) or (k == 0 and d == 1):
                arrived(G.at[k, 2, d], rB.at[k, d])
            for e in (1, 3):
                arrived(G.at[k, Y - e, d], rC.at[k, d, e // 2])

    acc[...] = jnp.zeros_like(acc)
    own_block(2)
    far_block(2)
    for e in range(1, MP):
        arrived(rawr.at[e - 1], r_raw.at[e - 1])
    raw = rawp[rows(mp * 32, 32)] + rawr[0] + rawr[1] + rawr[2]
    norm = jnp.sqrt(jnp.sum(raw * raw, axis=1, keepdims=True) + EPS)
    student = raw / norm
    st32[...] = student
    nm32[...] = jnp.broadcast_to(norm, (32, 128))
    own = rows(256 + q * 32, 32)
    stk[own] = student.astype(BF16)
    for e in range(1, LINE):
        push(stk.at[own], stk.at[own], s_stud.at[e - 1], r_stud.at[e - 1], line_peer(e))
    own_block(4)
    far_block(4)
    theirs = rows((1 - xl) * 128, 128)
    arrived(stk.at[theirs], r_tp.at[0])
    arrived(prow.at[1 - xl], r_tp.at[1])
    for i in range(XL):
        one = jnp.broadcast_to(prow[i][0:1].astype(F32), (128, 128))
        pcol[pl.ds(i * 128, 128)] = one.T
    own_block(6)
    for e in range(1, LINE):
        arrived(stk.at[rows(256 + rem(q - e, LINE) * 32, 32)], r_stud.at[e - 1])
    for k in (1, 2):
        complete(k)
        chunk(k)
    far_block(6)
    far()
    for k in (3, 4, 5, 6, 7, 0):
        complete(k)
        chunk(k)
        if k == 3:
            clip_t[...] = clip_v[...].T

    lane = lax.broadcasted_iota(jnp.int32, (256, 128), 1)
    cols = jnp.zeros((256, 128), F32)
    for i in range(4):
        cols = jnp.where(lane == i, jnp.sum(acc[i], axis=1, keepdims=True), cols)
    stat[...] = cols.T[0:8]
    for e in range(1, LINE):
        push(stat, statr.at[e - 1], s_stat.at[e - 1], r_stat.at[e - 1], line_peer(e))
    for e in range(1, LINE):
        arrived(statr.at[e - 1], r_stat.at[e - 1])
    sums = stat[...]
    for e in range(1, LINE):
        sums = sums + statr[e - 1]
    zt, zs, lean, pair = (sums[i : i + 1] for i in range(4))
    c_t = jnp.broadcast_to(1.0 / zt, (128, 256)).T
    c_s = jnp.broadcast_to(2.0 / zs, (128, 256)).T

    for k in range(8):
        hit = hits(k)
        for h in (0, 1):
            half = pl.ds(h * 128, 128)
            cf[:, k * 256 + h * 128 : k * 256 + (h + 1) * 128] = (
                ES[k, :, half] * c_s - ET[k, :, half] * c_t - hit[h].astype(F32)
            ).astype(BF16)
    dp[...] = jnp.dot(cf[...], G[...].reshape(2048, 512), preferred_element_type=F32)
    dpb[...] = dp[...].astype(BF16)
    for e in (3, 5, 4, 1, 7, 2, 6):
        other = rem(q + e, LINE)
        push(dpb.at[rows(other * 32, 32)], rsr.at[e - 1], s_rs.at[e - 1], r_rs.at[e - 1], line_peer(e))
    part = jnp.sum(lean / zt - jnp.log(zt) + 2.0 * jnp.log(zs) - pair, axis=1, keepdims=True)
    lossy[y] = jnp.broadcast_to(part, (1, 128))
    for e in range(1, Y):
        push(lossy.at[y], lossy.at[y], s_ly.at[e - 1], r_ly.at[e - 1], y_peer(e))
    for e in range(1, Y):
        arrived(lossy.at[rem(y - e, Y)], r_ly.at[e - 1])
    lossz[z] = lossy[0] + lossy[1] + lossy[2] + lossy[3]
    for e in range(1, Z):
        push(lossz.at[z], lossz.at[z], s_lz.at[e - 1], r_lz.at[e - 1], z_peer(e))
    dstud = dp[rows(q * 32, 32)]
    for e in range(1, LINE):
        arrived(rsr.at[e - 1], r_rs.at[e - 1])
        dstud = dstud + rsr[e - 1].astype(F32)
    dstud = dstud * (STUDENT_SCALE / total)
    student = st32[...]
    inner = jnp.sum(student * dstud, axis=1, keepdims=True)
    own = rows(mp * 32, 32)
    drw[own] = ((dstud - student * inner) / nm32[:, 0:1]).astype(BF16)
    for e in (2, 1, 3):
        push(drw.at[own], drw.at[own], s_dr.at[e - 1], r_dr.at[e - 1], mp_peer(e))
    for e in range(1, MP):
        arrived(drw.at[rows(rem(mp - e, MP) * 32, 32)], r_dr.at[e - 1])

    draw = drw[...]
    gs = jnp.dot(hid_t[...], draw, preferred_element_type=F32).astype(BF16)
    for jj in range(GROUP):
        for i in range(4):
            W[pl.ds(jj * SLICE + 96 + i * 16, 16)] = gs[jj * 16 : (jj + 1) * 16, i * 128 : (i + 1) * 128]

    def scatter(part, start, size):
        for e in range(1, GROUP):
            other, at = group_peer(e)
            src = W.at[pl.ds(pl.multiple_of(other * SLICE + start, 32), size)]
            push(src, p1.at[e - 1, pl.ds(start, size)], s_p1.at[part, e - 1], r_p1.at[part, e - 1], at)

    scatter(0, 96, 64)
    dpre = (dot_nt(draw, w2_v[...]) * gprime[...]).astype(BF16)
    gf = jnp.dot(clip_t[...], dpre, preferred_element_type=F32).astype(BF16)
    for jj in range(GROUP):
        W[pl.ds(jj * SLICE, 96)] = gf[jj * 96 : (jj + 1) * 96]
    scatter(1, 0, 96)

    def to_owner(t):
        owner = 8 * t // 5
        slot = rem(z - owner, Z) - 1
        tile = T.at[pl.ds(16 * t, 16)]
        return remote(tile, p2r.at[slot], s_p2.at[t], r_p2.at[slot], (y, owner, xl, mp))

    def summed(which, start, size):
        part = W[pl.ds(pl.multiple_of(j * SLICE + start, 32), size)].astype(F32)
        for e in range(1, GROUP):
            arrived(p1.at[e - 1, pl.ds(start, size)], r_p1.at[which, e - 1])
            part = part + p1[e - 1, start : start + size].astype(F32)
        own1[pl.ds(start, size)] = part
        T[pl.ds(start, size)] = part.astype(BF16)
        for t in range(start // 16, (start + size) // 16):

            @pl.when(z != 8 * t // 5)
            def _():
                to_owner(t).start()

    summed(0, 96, 64)
    summed(1, 0, 96)
    my_tile = lax.min((5 * z + 7) // 8, TILES - 1)
    owns = 8 * my_tile // 5 == z
    tile = rows(my_tile * 16, 16)

    @pl.when(owns)
    def _():
        out = own1[tile]
        for e in range(1, Z):
            arrived(p2r.at[e - 1], r_p2.at[e - 1])
            out = out + p2r[e - 1].astype(F32)
        R[tile] = out.astype(BF16)
        for e in range(1, Z):
            remote(R.at[tile], R.at[tile], s_p3.at[e - 1], r_p3.at[my_tile], z_peer(e)).start()

    for e in range(1, Z):
        arrived(lossz.at[rem(z - e, Z)], r_lz.at[e - 1])
    loss_sum = lossz[0]
    for i in range(1, Z):
        loss_sum = loss_sum + lossz[i]
    loss_o[0, 0] = jnp.sum(loss_sum[0:1, 0:1]) / total

    def tiles_arrived(first, last):
        for t in range(first, last):

            @pl.when(z != 8 * t // 5)
            def _():
                arrived(R.at[pl.ds(16 * t, 16)], r_p3.at[t])

    keep = []

    def give(i, src, dst):
        for e in range(1, GROUP):
            push(src, dst, s_p4.at[i, e - 1], r_p4.at[i, e - 1], group_peer(e)[1])
        keep.append(pltpu.make_async_copy(src, dst, sem_in.at[6 + i]))
        keep[-1].start()

    tiles_arrived(6, TILES)
    Rs[...] = jnp.concatenate([R[pl.ds(96 + i * 16, 16)] for i in range(4)], axis=1)
    give(1, Rs, gs_h.at[rows(j * 16, 16)])
    tiles_arrived(0, 6)
    give(0, R.at[pl.ds(0, 96)], gf_h.at[rows(j * 96, 96)])
    for copy in sends:
        copy.wait_send()
    for t in range(TILES):

        @pl.when(z != 8 * t // 5)
        def _():
            to_owner(t).wait_send()

    @pl.when(owns)
    def _():
        for e in range(1, Z):
            remote(R.at[tile], R.at[tile], s_p3.at[e - 1], s_p3.at[e - 1], me).wait_send()

    for copy in keep:
        copy.wait()
    for e in range(1, GROUP):
        other = rem(j - e, GROUP)
        arrived(gf_h.at[rows(other * 96, 96)], r_p4.at[0, e - 1])
        arrived(gs_h.at[rows(other * 16, 16)], r_p4.at[1, e - 1])


def body(clip_feats, teacher_audio, teacher_text, w_first, w_second, pairing):
    vm = pltpu.VMEM
    dma = pltpu.SemaphoreType.DMA
    hbm = pl.BlockSpec(memory_space=pl.ANY)
    scratch = [
        vm((128, 768), BF16), vm((128, 512), BF16), vm((32, 512), BF16),
        vm((768, 128), BF16), vm((128, 512), BF16), vm((1, 128), jnp.int32),
        vm((8, 4, 2, 32, 512), BF16),
        vm((512, 512), BF16), vm((2, 8, 128), jnp.int32), vm((256, 128), F32),
        vm((128, 512), F32), vm((3, 32, 512), F32), vm((32, 512), F32), vm((32, 128), F32),
        vm((128, 128), F32), vm((128, 128), BF16), vm((768, 128), BF16),
        vm((8, 256, 256), F32), vm((8, 256, 256), F32), vm((256, 2048), BF16), vm((4, 256, 128), F32),
        vm((8, 256), F32), vm((7, 8, 256), F32),
        vm((256, 512), F32), vm((256, 512), BF16), vm((7, 32, 512), BF16), vm((128, 512), BF16),
        vm((Y, 1, 128), F32), vm((Z, 1, 128), F32), vm((1280, 128), BF16),
        vm((GROUP - 1, SLICE, 128), BF16), vm((SLICE, 128), F32), vm((SLICE, 128), BF16),
        vm((Z - 1, 16, 128), BF16), vm((SLICE, 128), BF16), vm((16, 512), BF16),
        dma((8,)), dma((8, 2)), dma((8, 2)), dma((8, 2)), dma((8, 2)),
        dma((8, 2, 2)), dma((8, 2, 2)),
        dma((3,)), dma((3,)), dma((7,)), dma((7,)), dma((2,)), dma((2,)), dma((7,)), dma((7,)),
        dma((7,)), dma((7,)), dma((3,)), dma((3,)),
        dma((3,)), dma((3,)), dma((15,)), dma((15,)), dma((2, GROUP - 1)), dma((2, GROUP - 1)),
        dma((TILES,)), dma((Z - 1,)), dma((Z - 1,)), dma((TILES,)), dma((2, GROUP - 1)), dma((2, GROUP - 1)),
    ]
    loss, grad_first, grad_second = pl.pallas_call(
        kernel,
        out_shape=(
            jax.ShapeDtypeStruct((1, 1), F32),
            jax.ShapeDtypeStruct((768, 128), BF16),
            jax.ShapeDtypeStruct((128, 512), BF16),
        ),
        in_specs=[hbm] * 6,
        out_specs=(pl.BlockSpec(memory_space=pltpu.SMEM), hbm, hbm),
        scratch_shapes=scratch,
        compiler_params=pltpu.CompilerParams(
            collective_id=0, has_side_effects=True, vmem_limit_bytes=60 * 1024 * 1024
        ),
    )(clip_feats, teacher_audio, teacher_text, w_first, w_second, pairing.reshape(1, 128))
    grad_second, grad_first = lax.optimization_barrier((grad_second.astype(F32), grad_first))
    return loss.reshape(()), grad_first.astype(F32), grad_second


def solution(mesh):
    finer = Mesh(mesh.devices.reshape(Y, Z, XL, MP), ("y", "z", "xl", "mp"))
    return jax.shard_map(
        body,
        mesh=finer,
        in_specs=(
            P(WIDE, None),
            P(WIDE, None),
            P(WIDE + ("mp",), None),
            P(None, "mp"),
            P("mp", None),
            P(WIDE),
        ),
        out_specs=(P(), P(None, "mp"), P("mp", None)),
        check_vma=False,
    )
```

```python
import jax
import jax.numpy as jnp
from jax import lax
from jax.experimental import pallas as pl
from jax.experimental.pallas import tpu as pltpu
from jax.sharding import Mesh
from jax.sharding import PartitionSpec as P

MESH = pl.DeviceIdType.MESH
WIDE = ("y", "z", "xl")
F32 = jnp.float32
BF16 = jnp.bfloat16

Y, Z, XL, MP = 4, 16, 2, 4
LINE = XL * MP
TEACHER_SCALE = 14.0
STUDENT_SCALE = 64.0
EPS = 1e-6
GROUP = Y * XL
SLICE = 160
TILES = 10


def dot_nt(left, right):
    return lax.dot_general(
        left, right, (((1,), (1,)), ((), ())), preferred_element_type=F32
    )


def normalize(values):
    return values / jnp.sqrt(jnp.sum(values * values, axis=1, keepdims=True) + EPS)


def rows(start, size):
    return pl.ds(pl.multiple_of(start, size), size)


def kernel(
    clip_h, ta_h, tt_h, w1_h, w2_h, pair_h,
    loss_h, gf_h, gs_h,
    clip_v, ta_v, tt_v, w1_v, w2_v, pair_v,
    G, stk, prow, pcol, rawp, rawr, st32, nm32, gprime, hid_t, clip_t,
    ET, ES, cf, acc, stat, statr, dp, dpb, rsr, drw,
    lossy, lossz, W, p1, own1, T, p2r, R, Rs, loss_s,
    sem_in, sA, rA, sB, rB, sC, rC,
    s_raw, r_raw, s_stud, r_stud, s_tp, r_tp, s_stat, r_stat, s_rs, r_rs, s_dr, r_dr,
    s_ly, r_ly, s_lz, r_lz, s_p1, r_p1, s_p2, r_p2, s_p3, r_p3, s_p4, r_p4,
):
    y, z = lax.axis_index("y"), lax.axis_index("z")
    xl, mp = lax.axis_index("xl"), lax.axis_index("mp")
    q = xl * MP + mp
    j = y * XL + xl
    total = 128 * Y * Z * XL

    def rem(v, n):
        return lax.rem(v + 4 * n, n)

    def y_peer(e):
        return (rem(y + e, Y), z, xl, mp)

    def z_peer(e):
        return (y, rem(z + e, Z), xl, mp)

    def line_peer(e):
        other = rem(q + e, LINE)
        return (y, z, other // MP, rem(other, MP))

    def mp_peer(e):
        return (y, z, xl, rem(mp + e, MP))

    def group_peer(e):
        other = rem(j + e, GROUP)
        return other, (other // XL, z, rem(other, XL), mp)

    def remote(src, dst, send, recv, to):
        return pltpu.make_async_remote_copy(
            src_ref=src, dst_ref=dst, send_sem=send, recv_sem=recv, device_id=to,
            device_id_type=MESH,
        )

    me = (y, z, xl, mp)
    sends = []

    def push(*args):
        copy = remote(*args)
        copy.start()
        sends.append(copy)

    def arrived(dst, recv):
        remote(dst, dst, recv, recv, me).wait_recv()

    ins = [
        pltpu.make_async_copy(h, v, sem_in.at[i])
        for i, (h, v) in enumerate(
            [(tt_h, tt_v), (clip_h, clip_v), (w1_h, w1_v), (w2_h, w2_v), (ta_h, ta_v), (pair_h, pair_v)]
        )
    ]
    for c in ins:
        c.start()
    barrier = pltpu.get_barrier_semaphore()
    partners = [line_peer(e) for e in range(1, LINE)]
    partners += [y_peer(e) for e in range(1, Y)] + [z_peer(e) for e in (1, -1, 2, -2)]
    for p in partners:
        pl.semaphore_signal(barrier, inc=1, device_id=p, device_id_type=MESH)
    ins[0].wait()
    G[0, 0, 0] = normalize(tt_v[...].astype(F32)).astype(BF16)
    pl.semaphore_wait(barrier, len(partners))

    def along_z(o, k, d, send, recv):
        way = 1 - 2 * d
        for step in (2, 1):
            slot, side = k + step, d
            if slot == 8:
                if d != o // 2:
                    continue
                slot, side = 0, 1
            src = G.at[k, o, 0 if k == 0 else d]
            push(src, G.at[slot, o, side], send.at[slot, side], recv.at[slot, side], z_peer(way * step))

    def along_y(k, d):
        for e in (1, 3):
            push(G.at[k, 0, d], G.at[k, Y - e, d], sC.at[k, d, e // 2], rC.at[k, d, e // 2], y_peer(e))

    push(G.at[0, 0, 0], G.at[0, 2, 0], sB.at[0, 0], rB.at[0, 0], y_peer(2))
    for d in (0, 1):
        along_z(0, 0, d, sA, rA)
    along_y(0, 0)

    for c in ins[1:4]:
        c.wait()
    pre = jnp.dot(clip_v[...], w1_v[...], preferred_element_type=F32)
    cdf = 0.5 * (1.0 + lax.erf(pre * 0.7071067811865476))
    hid = (pre * cdf).astype(BF16)
    rawp[...] = jnp.dot(hid, w2_v[...], preferred_element_type=F32)
    for e in (2, 1, 3):
        other = rem(mp + e, MP)
        push(rawp.at[rows(other * 32, 32)], rawr.at[e - 1], s_raw.at[e - 1], r_raw.at[e - 1], mp_peer(e))
    arrived(G.at[0, 2, 0], rB.at[0, 0])
    for d in (0, 1):
        along_z(2, 0, d, sB, rB)
    ins[4].wait()
    ins[5].wait()
    mine = rows(xl * 128, 128)
    stk[mine] = normalize(ta_v[...].astype(F32)).astype(BF16)
    prow[xl] = jnp.broadcast_to(pair_v[...], (8, 128))
    other_x = (y, z, 1 - xl, mp)
    push(stk.at[mine], stk.at[mine], s_tp.at[0], r_tp.at[0], other_x)
    push(prow.at[xl], prow.at[xl], s_tp.at[1], r_tp.at[1], other_x)
    gprime[...] = cdf + pre * (0.3989422804014327 * jnp.exp(-0.5 * pre * pre))
    hid_t[...] = hid.T

    def own_block(k):
        for d in (0, 1):
            arrived(G.at[k, 0, d], rA.at[k, d])
            along_z(0, k, d, sA, rA)
        for d in (0, 1):
            along_y(k, d)
        for d in (0, 1):
            arrived(G.at[k - 1, 0, d], rA.at[k - 1, d])
            along_y(k - 1, d)

    def far_block(k):
        for d in (0, 1):
            arrived(G.at[k, 2, d], rB.at[k, d])
            along_z(2, k, d, sB, rB)

    def far():
        for k, d in ((7, 0), (7, 1), (0, 1)):
            arrived(G.at[k, 0, d], rA.at[k, d])
            along_y(k, d)

    col = lax.broadcasted_iota(jnp.int32, (8, 256), 1)
    way = (col // 32) & 1
    y_at = (y + col // 64) & (Y - 1)
    id_base = ((y_at * Z) * XL + xl) * 128 + mp * 32 + (col & 31)

    def hits(k):
        z_left = rem(z - k, Z)
        z_right = jnp.where(k == 0, rem(z + 8, Z), rem(z + k, Z))
        ids = id_base + jnp.where(way == 1, z_right, z_left) * (XL * 128)
        ids = ids[0:1].astype(F32)
        return [pcol[...] == ids[:, h * 128 : (h + 1) * 128] for h in (0, 1)]

    def captions(k):
        return G[k].reshape(256, 512)

    def chunk(k):
        scores = dot_nt(stk[...], captions(k))
        tlog = TEACHER_SCALE * scores[:256]
        slog = STUDENT_SCALE * scores[256:]
        texp, sexp = jnp.exp(tlog), jnp.exp(slog)
        ET[k] = texp
        ES[k] = sexp
        lean = texp * (tlog - slog)
        hit = hits(k)
        pair = [jnp.where(hit[h], slog[:, h * 128 : (h + 1) * 128], 0.0) for h in (0, 1)]
        acc[0] += texp[:, :128] + texp[:, 128:]
        acc[1] += sexp[:, :128] + sexp[:, 128:]
        acc[2] += lean[:, :128] + lean[:, 128:]
        acc[3] += pair[0] + pair[1]

    def complete(k):
        for d in (0, 1):
            if k == 7 or (k in (1, 3, 5)) or (k == 0 and d == 1):
                arrived(G.at[k, 2, d], rB.at[k, d])
            for e in (1, 3):
                arrived(G.at[k, Y - e, d], rC.at[k, d, e // 2])

    acc[...] = jnp.zeros_like(acc)
    own_block(2)
    far_block(2)
    for e in range(1, MP):
        arrived(rawr.at[e - 1], r_raw.at[e - 1])
    raw = rawp[rows(mp * 32, 32)] + rawr[0] + rawr[1] + rawr[2]
    norm = jnp.sqrt(jnp.sum(raw * raw, axis=1, keepdims=True) + EPS)
    student = raw / norm
    st32[...] = student
    nm32[...] = jnp.broadcast_to(norm, (32, 128))
    own = rows(256 + q * 32, 32)
    stk[own] = student.astype(BF16)
    for e in range(1, LINE):
        push(stk.at[own], stk.at[own], s_stud.at[e - 1], r_stud.at[e - 1], line_peer(e))
    own_block(4)
    far_block(4)
    theirs = rows((1 - xl) * 128, 128)
    arrived(stk.at[theirs], r_tp.at[0])
    arrived(prow.at[1 - xl], r_tp.at[1])
    for i in range(XL):
        one = jnp.broadcast_to(prow[i][0:1].astype(F32), (128, 128))
        pcol[pl.ds(i * 128, 128)] = one.T
    own_block(6)
    for e in range(1, LINE):
        arrived(stk.at[rows(256 + rem(q - e, LINE) * 32, 32)], r_stud.at[e - 1])
    for k in (1, 2):
        complete(k)
        chunk(k)
    far_block(6)
    far()
    for k in (3, 4, 5, 6, 7, 0):
        complete(k)
        chunk(k)
        if k == 3:
            clip_t[...] = clip_v[...].T

    lane = lax.broadcasted_iota(jnp.int32, (256, 128), 1)
    cols = jnp.zeros((256, 128), F32)
    for i in range(4):
        cols = jnp.where(lane == i, jnp.sum(acc[i], axis=1, keepdims=True), cols)
    stat[...] = cols.T[0:8]
    for e in range(1, LINE):
        push(stat, statr.at[e - 1], s_stat.at[e - 1], r_stat.at[e - 1], line_peer(e))
    for e in range(1, LINE):
        arrived(statr.at[e - 1], r_stat.at[e - 1])
    sums = stat[...]
    for e in range(1, LINE):
        sums = sums + statr[e - 1]
    zt, zs, lean, pair = (sums[i : i + 1] for i in range(4))
    c_t = jnp.broadcast_to(1.0 / zt, (128, 256)).T
    c_s = jnp.broadcast_to(2.0 / zs, (128, 256)).T

    for k in range(8):
        hit = hits(k)
        for h in (0, 1):
            half = pl.ds(h * 128, 128)
            cf[:, k * 256 + h * 128 : k * 256 + (h + 1) * 128] = (
                ES[k, :, half] * c_s - ET[k, :, half] * c_t - hit[h].astype(F32)
            ).astype(BF16)
    dp[...] = jnp.dot(cf[...], G[...].reshape(2048, 512), preferred_element_type=F32)
    dpb[...] = dp[...].astype(BF16)
    for e in (3, 5, 4, 1, 7, 2, 6):
        other = rem(q + e, LINE)
        push(dpb.at[rows(other * 32, 32)], rsr.at[e - 1], s_rs.at[e - 1], r_rs.at[e - 1], line_peer(e))
    part = jnp.sum(lean / zt - jnp.log(zt) + 2.0 * jnp.log(zs) - pair, axis=1, keepdims=True)
    lossy[y] = jnp.broadcast_to(part, (1, 128))
    for e in range(1, Y):
        push(lossy.at[y], lossy.at[y], s_ly.at[e - 1], r_ly.at[e - 1], y_peer(e))
    for e in range(1, Y):
        arrived(lossy.at[rem(y - e, Y)], r_ly.at[e - 1])
    lossz[z] = lossy[0] + lossy[1] + lossy[2] + lossy[3]
    for e in range(1, Z):
        push(lossz.at[z], lossz.at[z], s_lz.at[e - 1], r_lz.at[e - 1], z_peer(e))
    dstud = dp[rows(q * 32, 32)]
    for e in range(1, LINE):
        arrived(rsr.at[e - 1], r_rs.at[e - 1])
        dstud = dstud + rsr[e - 1].astype(F32)
    dstud = dstud * (STUDENT_SCALE / total)
    student = st32[...]
    inner = jnp.sum(student * dstud, axis=1, keepdims=True)
    own = rows(mp * 32, 32)
    drw[own] = ((dstud - student * inner) / nm32[:, 0:1]).astype(BF16)
    for e in (2, 1, 3):
        push(drw.at[own], drw.at[own], s_dr.at[e - 1], r_dr.at[e - 1], mp_peer(e))
    for e in range(1, MP):
        arrived(drw.at[rows(rem(mp - e, MP) * 32, 32)], r_dr.at[e - 1])

    draw = drw[...]
    gs = jnp.dot(hid_t[...], draw, preferred_element_type=F32).astype(BF16)
    for jj in range(GROUP):
        for i in range(4):
            W[pl.ds(jj * SLICE + 96 + i * 16, 16)] = gs[jj * 16 : (jj + 1) * 16, i * 128 : (i + 1) * 128]

    def scatter(part, start, size):
        for e in range(1, GROUP):
            other, at = group_peer(e)
            src = W.at[pl.ds(pl.multiple_of(other * SLICE + start, 32), size)]
            push(src, p1.at[e - 1, pl.ds(start, size)], s_p1.at[part, e - 1], r_p1.at[part, e - 1], at)

    scatter(0, 96, 64)
    dpre = (dot_nt(draw, w2_v[...]) * gprime[...]).astype(BF16)
    gf = jnp.dot(clip_t[...], dpre, preferred_element_type=F32).astype(BF16)
    for jj in range(GROUP):
        W[pl.ds(jj * SLICE, 96)] = gf[jj * 96 : (jj + 1) * 96]
    scatter(1, 0, 96)

    def to_owner(t):
        owner = 8 * t // 5
        slot = rem(z - owner, Z) - 1
        tile = T.at[pl.ds(16 * t, 16)]
        return remote(tile, p2r.at[slot], s_p2.at[t], r_p2.at[slot], (y, owner, xl, mp))

    def summed(which, start, size):
        part = W[pl.ds(pl.multiple_of(j * SLICE + start, 32), size)].astype(F32)
        for e in range(1, GROUP):
            arrived(p1.at[e - 1, pl.ds(start, size)], r_p1.at[which, e - 1])
            part = part + p1[e - 1, start : start + size].astype(F32)
        own1[pl.ds(start, size)] = part
        T[pl.ds(start, size)] = part.astype(BF16)
        for t in range(start // 16, (start + size) // 16):

            @pl.when(z != 8 * t // 5)
            def _():
                to_owner(t).start()

    summed(0, 96, 64)
    summed(1, 0, 96)
    my_tile = lax.min((5 * z + 7) // 8, TILES - 1)
    owns = 8 * my_tile // 5 == z
    tile = rows(my_tile * 16, 16)

    @pl.when(owns)
    def _():
        out = own1[tile]
        for e in range(1, Z):
            arrived(p2r.at[e - 1], r_p2.at[e - 1])
            out = out + p2r[e - 1].astype(F32)
        R[tile] = out.astype(BF16)
        for e in range(1, Z):
            remote(R.at[tile], R.at[tile], s_p3.at[e - 1], r_p3.at[my_tile], z_peer(e)).start()

    for e in range(1, Z):
        arrived(lossz.at[rem(z - e, Z)], r_lz.at[e - 1])
    loss_sum = lossz[0]
    for i in range(1, Z):
        loss_sum = loss_sum + lossz[i]
    loss_s[0, 0] = jnp.sum(loss_sum[0:1, 0:1]) / total
    keep = [pltpu.make_async_copy(loss_s, loss_h, sem_in.at[8])]
    keep[0].start()

    def tiles_arrived(first, last):
        for t in range(first, last):

            @pl.when(z != 8 * t // 5)
            def _():
                arrived(R.at[pl.ds(16 * t, 16)], r_p3.at[t])

    def give(i, src, dst):
        for e in range(1, GROUP):
            push(src, dst, s_p4.at[i, e - 1], r_p4.at[i, e - 1], group_peer(e)[1])
        keep.append(pltpu.make_async_copy(src, dst, sem_in.at[6 + i]))
        keep[-1].start()

    tiles_arrived(6, TILES)
    Rs[...] = jnp.concatenate([R[pl.ds(96 + i * 16, 16)] for i in range(4)], axis=1)
    give(1, Rs, gs_h.at[rows(j * 16, 16)])
    tiles_arrived(0, 6)
    give(0, R.at[pl.ds(0, 96)], gf_h.at[rows(j * 96, 96)])
    for copy in sends:
        copy.wait_send()
    for t in range(TILES):

        @pl.when(z != 8 * t // 5)
        def _():
            to_owner(t).wait_send()

    @pl.when(owns)
    def _():
        for e in range(1, Z):
            remote(R.at[tile], R.at[tile], s_p3.at[e - 1], s_p3.at[e - 1], me).wait_send()

    for copy in keep:
        copy.wait()
    for e in range(1, GROUP):
        other = rem(j - e, GROUP)
        arrived(gf_h.at[rows(other * 96, 96)], r_p4.at[0, e - 1])
        arrived(gs_h.at[rows(other * 16, 16)], r_p4.at[1, e - 1])


def body(clip_feats, teacher_audio, teacher_text, w_first, w_second, pairing):
    vm = pltpu.VMEM
    dma = pltpu.SemaphoreType.DMA
    hbm = pl.BlockSpec(memory_space=pl.ANY)
    scratch = [
        vm((128, 768), BF16), vm((128, 512), BF16), vm((32, 512), BF16),
        vm((768, 128), BF16), vm((128, 512), BF16), vm((1, 128), jnp.int32),
        vm((8, 4, 2, 32, 512), BF16),
        vm((512, 512), BF16), vm((2, 8, 128), jnp.int32), vm((256, 128), F32),
        vm((128, 512), F32), vm((3, 32, 512), F32), vm((32, 512), F32), vm((32, 128), F32),
        vm((128, 128), F32), vm((128, 128), BF16), vm((768, 128), BF16),
        vm((8, 256, 256), F32), vm((8, 256, 256), F32), vm((256, 2048), BF16), vm((4, 256, 128), F32),
        vm((8, 256), F32), vm((7, 8, 256), F32),
        vm((256, 512), F32), vm((256, 512), BF16), vm((7, 32, 512), BF16), vm((128, 512), BF16),
        vm((Y, 1, 128), F32), vm((Z, 1, 128), F32), vm((1280, 128), BF16),
        vm((GROUP - 1, SLICE, 128), BF16), vm((SLICE, 128), F32), vm((SLICE, 128), BF16),
        vm((Z - 1, 16, 128), BF16), vm((SLICE, 128), BF16), vm((16, 512), BF16), pltpu.SMEM((1, 1), F32),
        dma((9,)), dma((8, 2)), dma((8, 2)), dma((8, 2)), dma((8, 2)),
        dma((8, 2, 2)), dma((8, 2, 2)),
        dma((3,)), dma((3,)), dma((7,)), dma((7,)), dma((2,)), dma((2,)), dma((7,)), dma((7,)),
        dma((7,)), dma((7,)), dma((3,)), dma((3,)),
        dma((3,)), dma((3,)), dma((15,)), dma((15,)), dma((2, GROUP - 1)), dma((2, GROUP - 1)),
        dma((TILES,)), dma((Z - 1,)), dma((Z - 1,)), dma((TILES,)), dma((2, GROUP - 1)), dma((2, GROUP - 1)),
    ]
    loss, grad_first, grad_second = pl.pallas_call(
        kernel,
        out_shape=(
            jax.ShapeDtypeStruct((1, 1), F32),
            jax.ShapeDtypeStruct((768, 128), BF16),
            jax.ShapeDtypeStruct((128, 512), BF16),
        ),
        in_specs=[hbm] * 6,
        out_specs=(hbm, hbm, hbm),
        scratch_shapes=scratch,
        compiler_params=pltpu.CompilerParams(
            collective_id=0, has_side_effects=True, vmem_limit_bytes=32 * 1024 * 1024
        ),
    )(*(pltpu.with_memory_space_constraint(a, pltpu.HBM) for a in (clip_feats, teacher_audio, teacher_text, w_first, w_second, pairing.reshape(1, 128))))
    grad_second, grad_first = lax.optimization_barrier((grad_second.astype(F32), grad_first))
    return loss.reshape(()), grad_first.astype(F32), grad_second


def solution(mesh):
    finer = Mesh(mesh.devices.reshape(Y, Z, XL, MP), ("y", "z", "xl", "mp"))
    return jax.shard_map(
        body,
        mesh=finer,
        in_specs=(
            P(WIDE, None),
            P(WIDE, None),
            P(WIDE + ("mp",), None),
            P(None, "mp"),
            P("mp", None),
            P(WIDE),
        ),
        out_specs=(P(), P(None, "mp"), P("mp", None)),
        check_vma=False,
    )
```

```python
import jax
import jax.numpy as jnp
from jax import lax
from jax.experimental import pallas as pl
from jax.experimental.pallas import tpu as pltpu
from jax.sharding import Mesh
from jax.sharding import PartitionSpec as P

MESH = pl.DeviceIdType.MESH
WIDE = ("y", "z", "xl")
F32 = jnp.float32
BF16 = jnp.bfloat16

Y, Z, XL, MP = 4, 16, 2, 4
LINE = XL * MP
TEACHER_SCALE = 14.0
STUDENT_SCALE = 64.0
EPS = 1e-6
GROUP = Y * XL
SLICE = 160
TILES = 10


def dot_nt(left, right):
    return lax.dot_general(
        left, right, (((1,), (1,)), ((), ())), preferred_element_type=F32
    )


def normalize(values):
    return values / jnp.sqrt(jnp.sum(values * values, axis=1, keepdims=True) + EPS)


def far_first(size):
    return sorted(range(1, size), key=lambda e: -min(e, size - e))


def rows(start, size):
    return pl.ds(pl.multiple_of(start, size), size)


def kernel(
    clip_h, ta_h, tt_h, w1_h, w2_h, pair_h,
    loss_h, gf_h, gs_h,
    clip_v, ta_v, tt_v, w1_v, w2_v, pair_v,
    G, stk, prow, pcol, rawp, rawr, st32, nm32, gprime, hid_t, clip_t,
    ET, ES, cf, acc, stat, statr, dp, dpb, rsr, drw,
    lossy, lossz, W, p1, own1, T, p2r, R, Rs, loss_s,
    sem_in, sA, rA, sB, rB, sC, rC,
    s_raw, r_raw, s_stud, r_stud, s_tp, r_tp, s_stat, r_stat, s_rs, r_rs, s_dr, r_dr,
    s_ly, r_ly, s_lz, r_lz, s_p1, r_p1, s_p2, r_p2, s_p3, r_p3, s_p4, r_p4,
):
    y, z = lax.axis_index("y"), lax.axis_index("z")
    xl, mp = lax.axis_index("xl"), lax.axis_index("mp")
    q = xl * MP + mp
    j = y * XL + xl
    total = 128 * Y * Z * XL

    def rem(v, n):
        return lax.rem(v + 4 * n, n)

    def y_peer(e):
        return (rem(y + e, Y), z, xl, mp)

    def z_peer(e):
        return (y, rem(z + e, Z), xl, mp)

    def line_peer(e):
        other = rem(q + e, LINE)
        return (y, z, other // MP, rem(other, MP))

    def mp_peer(e):
        return (y, z, xl, rem(mp + e, MP))

    def group_peer(e):
        other = rem(j + e, GROUP)
        return other, (other // XL, z, rem(other, XL), mp)

    def remote(src, dst, send, recv, to):
        return pltpu.make_async_remote_copy(
            src_ref=src, dst_ref=dst, send_sem=send, recv_sem=recv, device_id=to,
            device_id_type=MESH,
        )

    me = (y, z, xl, mp)
    sends = []

    def push(*args):
        copy = remote(*args)
        copy.start()
        sends.append(copy)

    def arrived(dst, recv):
        remote(dst, dst, recv, recv, me).wait_recv()

    ins = [
        pltpu.make_async_copy(h, v, sem_in.at[i])
        for i, (h, v) in enumerate(
            [(tt_h, tt_v), (clip_h, clip_v), (w1_h, w1_v), (w2_h, w2_v), (ta_h, ta_v), (pair_h, pair_v)]
        )
    ]
    for c in ins:
        c.start()
    barrier = pltpu.get_barrier_semaphore()
    partners = [line_peer(e) for e in range(1, LINE)]
    partners += [y_peer(e) for e in range(1, Y)] + [z_peer(e) for e in (1, -1, 2, -2)]
    for p in partners:
        pl.semaphore_signal(barrier, inc=1, device_id=p, device_id_type=MESH)
    ins[0].wait()
    G[0, 0, 0] = normalize(tt_v[...].astype(F32)).astype(BF16)
    pl.semaphore_wait(barrier, len(partners))

    def along_z(o, k, d, send, recv):
        way = 1 - 2 * d
        for step in (2, 1):
            slot, side = k + step, d
            if slot == 8:
                if d != o // 2:
                    continue
                slot, side = 0, 1
            src = G.at[k, o, 0 if k == 0 else d]
            push(src, G.at[slot, o, side], send.at[slot, side], recv.at[slot, side], z_peer(way * step))

    def along_y(k, d):
        for e in (1, 3):
            push(G.at[k, 0, d], G.at[k, Y - e, d], sC.at[k, d, e // 2], rC.at[k, d, e // 2], y_peer(e))

    push(G.at[0, 0, 0], G.at[0, 2, 0], sB.at[0, 0], rB.at[0, 0], y_peer(2))
    for d in (0, 1):
        along_z(0, 0, d, sA, rA)
    along_y(0, 0)

    for c in ins[1:4]:
        c.wait()
    pre = jnp.dot(clip_v[...], w1_v[...], preferred_element_type=F32)
    cdf = 0.5 * (1.0 + lax.erf(pre * 0.7071067811865476))
    hid = (pre * cdf).astype(BF16)
    rawp[...] = jnp.dot(hid, w2_v[...], preferred_element_type=F32)
    for e in (2, 1, 3):
        other = rem(mp + e, MP)
        push(rawp.at[rows(other * 32, 32)], rawr.at[e - 1], s_raw.at[e - 1], r_raw.at[e - 1], mp_peer(e))
    arrived(G.at[0, 2, 0], rB.at[0, 0])
    for d in (0, 1):
        along_z(2, 0, d, sB, rB)
    ins[4].wait()
    ins[5].wait()
    mine = rows(xl * 128, 128)
    stk[mine] = normalize(ta_v[...].astype(F32)).astype(BF16)
    prow[xl] = jnp.broadcast_to(pair_v[...], (8, 128))
    other_x = (y, z, 1 - xl, mp)
    push(stk.at[mine], stk.at[mine], s_tp.at[0], r_tp.at[0], other_x)
    push(prow.at[xl], prow.at[xl], s_tp.at[1], r_tp.at[1], other_x)
    gprime[...] = cdf + pre * (0.3989422804014327 * jnp.exp(-0.5 * pre * pre))
    hid_t[...] = hid.T

    def own_block(k):
        for d in (0, 1):
            arrived(G.at[k, 0, d], rA.at[k, d])
            along_z(0, k, d, sA, rA)
        for d in (0, 1):
            along_y(k, d)
        for d in (0, 1):
            arrived(G.at[k - 1, 0, d], rA.at[k - 1, d])
            along_y(k - 1, d)

    def far_block(k):
        for d in (0, 1):
            arrived(G.at[k, 2, d], rB.at[k, d])
            along_z(2, k, d, sB, rB)

    def far():
        for k, d in ((7, 0), (7, 1), (0, 1)):
            arrived(G.at[k, 0, d], rA.at[k, d])
            along_y(k, d)

    col = lax.broadcasted_iota(jnp.int32, (8, 256), 1)
    way = (col // 32) & 1
    y_at = (y + col // 64) & (Y - 1)
    id_base = ((y_at * Z) * XL + xl) * 128 + mp * 32 + (col & 31)

    def hits(k):
        z_left = rem(z - k, Z)
        z_right = jnp.where(k == 0, rem(z + 8, Z), rem(z + k, Z))
        ids = id_base + jnp.where(way == 1, z_right, z_left) * (XL * 128)
        ids = ids[0:1].astype(F32)
        return [pcol[...] == ids[:, h * 128 : (h + 1) * 128] for h in (0, 1)]

    def captions(k):
        return G[k].reshape(256, 512)

    def chunk(k):
        scores = dot_nt(stk[...], captions(k))
        tlog = TEACHER_SCALE * scores[:256]
        slog = STUDENT_SCALE * scores[256:]
        texp, sexp = jnp.exp(tlog), jnp.exp(slog)
        ET[k] = texp
        ES[k] = sexp
        lean = texp * (tlog - slog)
        hit = hits(k)
        pair = [jnp.where(hit[h], slog[:, h * 128 : (h + 1) * 128], 0.0) for h in (0, 1)]
        acc[0] += texp[:, :128] + texp[:, 128:]
        acc[1] += sexp[:, :128] + sexp[:, 128:]
        acc[2] += lean[:, :128] + lean[:, 128:]
        acc[3] += pair[0] + pair[1]

    def complete(k):
        for d in (0, 1):
            if k == 7 or (k in (1, 3, 5)) or (k == 0 and d == 1):
                arrived(G.at[k, 2, d], rB.at[k, d])
            for e in (1, 3):
                arrived(G.at[k, Y - e, d], rC.at[k, d, e // 2])

    acc[...] = jnp.zeros_like(acc)
    own_block(2)
    far_block(2)
    for e in range(1, MP):
        arrived(rawr.at[e - 1], r_raw.at[e - 1])
    raw = rawp[rows(mp * 32, 32)] + rawr[0] + rawr[1] + rawr[2]
    norm = jnp.sqrt(jnp.sum(raw * raw, axis=1, keepdims=True) + EPS)
    student = raw / norm
    st32[...] = student
    nm32[...] = jnp.broadcast_to(norm, (32, 128))
    own = rows(256 + q * 32, 32)
    stk[own] = student.astype(BF16)
    for e in range(1, LINE):
        push(stk.at[own], stk.at[own], s_stud.at[e - 1], r_stud.at[e - 1], line_peer(e))
    own_block(4)
    far_block(4)
    theirs = rows((1 - xl) * 128, 128)
    arrived(stk.at[theirs], r_tp.at[0])
    arrived(prow.at[1 - xl], r_tp.at[1])
    for i in range(XL):
        one = jnp.broadcast_to(prow[i][0:1].astype(F32), (128, 128))
        pcol[pl.ds(i * 128, 128)] = one.T
    own_block(6)
    for e in range(1, LINE):
        arrived(stk.at[rows(256 + rem(q - e, LINE) * 32, 32)], r_stud.at[e - 1])
    for k in (1, 2):
        complete(k)
        chunk(k)
    far_block(6)
    far()
    for k in (3, 4, 5, 6, 7, 0):
        complete(k)
        chunk(k)
        if k == 3:
            clip_t[...] = clip_v[...].T

    lane = lax.broadcasted_iota(jnp.int32, (256, 128), 1)
    cols = jnp.zeros((256, 128), F32)
    for i in range(4):
        cols = jnp.where(lane == i, jnp.sum(acc[i], axis=1, keepdims=True), cols)
    stat[...] = cols.T[0:8]
    for e in range(1, LINE):
        push(stat, statr.at[e - 1], s_stat.at[e - 1], r_stat.at[e - 1], line_peer(e))
    for e in range(1, LINE):
        arrived(statr.at[e - 1], r_stat.at[e - 1])
    sums = stat[...]
    for e in range(1, LINE):
        sums = sums + statr[e - 1]
    zt, zs, lean, pair = (sums[i : i + 1] for i in range(4))
    c_t = jnp.broadcast_to(1.0 / zt, (128, 256)).T
    c_s = jnp.broadcast_to(2.0 / zs, (128, 256)).T

    for k in range(8):
        hit = hits(k)
        for h in (0, 1):
            half = pl.ds(h * 128, 128)
            cf[:, k * 256 + h * 128 : k * 256 + (h + 1) * 128] = (
                ES[k, :, half] * c_s - ET[k, :, half] * c_t - hit[h].astype(F32)
            ).astype(BF16)
    dp[...] = jnp.dot(cf[...], G[...].reshape(2048, 512), preferred_element_type=F32)
    dpb[...] = dp[...].astype(BF16)
    for e in (3, 5, 4, 1, 7, 2, 6):
        other = rem(q + e, LINE)
        push(dpb.at[rows(other * 32, 32)], rsr.at[e - 1], s_rs.at[e - 1], r_rs.at[e - 1], line_peer(e))
    part = jnp.sum(lean / zt - jnp.log(zt) + 2.0 * jnp.log(zs) - pair, axis=1, keepdims=True)
    lossy[y] = jnp.broadcast_to(part, (1, 128))
    for e in range(1, Y):
        push(lossy.at[y], lossy.at[y], s_ly.at[e - 1], r_ly.at[e - 1], y_peer(e))
    for e in range(1, Y):
        arrived(lossy.at[rem(y - e, Y)], r_ly.at[e - 1])
    lossz[z] = lossy[0] + lossy[1] + lossy[2] + lossy[3]
    for e in range(1, Z):
        push(lossz.at[z], lossz.at[z], s_lz.at[e - 1], r_lz.at[e - 1], z_peer(e))
    dstud = dp[rows(q * 32, 32)]
    for e in range(1, LINE):
        arrived(rsr.at[e - 1], r_rs.at[e - 1])
        dstud = dstud + rsr[e - 1].astype(F32)
    dstud = dstud * (STUDENT_SCALE / total)
    student = st32[...]
    inner = jnp.sum(student * dstud, axis=1, keepdims=True)
    own = rows(mp * 32, 32)
    drw[own] = ((dstud - student * inner) / nm32[:, 0:1]).astype(BF16)
    for e in (2, 1, 3):
        push(drw.at[own], drw.at[own], s_dr.at[e - 1], r_dr.at[e - 1], mp_peer(e))
    for e in range(1, MP):
        arrived(drw.at[rows(rem(mp - e, MP) * 32, 32)], r_dr.at[e - 1])

    draw = drw[...]
    gs = jnp.dot(hid_t[...], draw, preferred_element_type=F32).astype(BF16)
    for jj in range(GROUP):
        for i in range(4):
            W[pl.ds(jj * SLICE + 96 + i * 16, 16)] = gs[jj * 16 : (jj + 1) * 16, i * 128 : (i + 1) * 128]

    def scatter(part, start, size):
        for e in far_first(GROUP):
            other, at = group_peer(e)
            src = W.at[pl.ds(pl.multiple_of(other * SLICE + start, 32), size)]
            push(src, p1.at[e - 1, pl.ds(start, size)], s_p1.at[part, e - 1], r_p1.at[part, e - 1], at)

    scatter(0, 96, 64)
    dpre = (dot_nt(draw, w2_v[...]) * gprime[...]).astype(BF16)
    gf = jnp.dot(clip_t[...], dpre, preferred_element_type=F32).astype(BF16)
    for jj in range(GROUP):
        W[pl.ds(jj * SLICE, 96)] = gf[jj * 96 : (jj + 1) * 96]
    scatter(1, 0, 96)

    def to_owner(t):
        owner = 8 * t // 5
        slot = rem(z - owner, Z) - 1
        tile = T.at[pl.ds(16 * t, 16)]
        return remote(tile, p2r.at[slot], s_p2.at[t], r_p2.at[slot], (y, owner, xl, mp))

    def summed(which, start, size):
        part = W[pl.ds(pl.multiple_of(j * SLICE + start, 32), size)].astype(F32)
        for e in range(1, GROUP):
            arrived(p1.at[e - 1, pl.ds(start, size)], r_p1.at[which, e - 1])
            part = part + p1[e - 1, start : start + size].astype(F32)
        own1[pl.ds(start, size)] = part
        T[pl.ds(start, size)] = part.astype(BF16)
        for t in range(start // 16, (start + size) // 16):

            @pl.when(z != 8 * t // 5)
            def _():
                to_owner(t).start()

    summed(0, 96, 64)
    summed(1, 0, 96)
    my_tile = lax.min((5 * z + 7) // 8, TILES - 1)
    owns = 8 * my_tile // 5 == z
    tile = rows(my_tile * 16, 16)

    @pl.when(owns)
    def _():
        out = own1[tile]
        for e in range(1, Z):
            arrived(p2r.at[e - 1], r_p2.at[e - 1])
            out = out + p2r[e - 1].astype(F32)
        R[tile] = out.astype(BF16)
        for e in far_first(Z):
            remote(R.at[tile], R.at[tile], s_p3.at[e - 1], r_p3.at[my_tile], z_peer(e)).start()

    for e in range(1, Z):
        arrived(lossz.at[rem(z - e, Z)], r_lz.at[e - 1])
    loss_sum = lossz[0]
    for i in range(1, Z):
        loss_sum = loss_sum + lossz[i]
    loss_s[0, 0] = jnp.sum(loss_sum[0:1, 0:1]) / total
    keep = [pltpu.make_async_copy(loss_s, loss_h, sem_in.at[8])]
    keep[0].start()

    def tiles_arrived(first, last):
        for t in range(first, last):

            @pl.when(z != 8 * t // 5)
            def _():
                arrived(R.at[pl.ds(16 * t, 16)], r_p3.at[t])

    def give(i, src, dst):
        for e in far_first(GROUP):
            push(src, dst, s_p4.at[i, e - 1], r_p4.at[i, e - 1], group_peer(e)[1])
        keep.append(pltpu.make_async_copy(src, dst, sem_in.at[6 + i]))
        keep[-1].start()

    tiles_arrived(6, TILES)
    Rs[...] = jnp.concatenate([R[pl.ds(96 + i * 16, 16)] for i in range(4)], axis=1)
    give(1, Rs, gs_h.at[rows(j * 16, 16)])
    tiles_arrived(0, 6)
    give(0, R.at[pl.ds(0, 96)], gf_h.at[rows(j * 96, 96)])
    for copy in sends:
        copy.wait_send()
    for t in range(TILES):

        @pl.when(z != 8 * t // 5)
        def _():
            to_owner(t).wait_send()

    @pl.when(owns)
    def _():
        for e in range(1, Z):
            remote(R.at[tile], R.at[tile], s_p3.at[e - 1], s_p3.at[e - 1], me).wait_send()

    for copy in keep:
        copy.wait()
    for e in range(1, GROUP):
        other = rem(j - e, GROUP)
        arrived(gf_h.at[rows(other * 96, 96)], r_p4.at[0, e - 1])
        arrived(gs_h.at[rows(other * 16, 16)], r_p4.at[1, e - 1])


def body(clip_feats, teacher_audio, teacher_text, w_first, w_second, pairing):
    vm = pltpu.VMEM
    dma = pltpu.SemaphoreType.DMA
    hbm = pl.BlockSpec(memory_space=pl.ANY)
    scratch = [
        vm((128, 768), BF16), vm((128, 512), BF16), vm((32, 512), BF16),
        vm((768, 128), BF16), vm((128, 512), BF16), vm((1, 128), jnp.int32),
        vm((8, 4, 2, 32, 512), BF16),
        vm((512, 512), BF16), vm((2, 8, 128), jnp.int32), vm((256, 128), F32),
        vm((128, 512), F32), vm((3, 32, 512), F32), vm((32, 512), F32), vm((32, 128), F32),
        vm((128, 128), F32), vm((128, 128), BF16), vm((768, 128), BF16),
        vm((8, 256, 256), F32), vm((8, 256, 256), F32), vm((256, 2048), BF16), vm((4, 256, 128), F32),
        vm((8, 256), F32), vm((7, 8, 256), F32),
        vm((256, 512), F32), vm((256, 512), BF16), vm((7, 32, 512), BF16), vm((128, 512), BF16),
        vm((Y, 1, 128), F32), vm((Z, 1, 128), F32), vm((1280, 128), BF16),
        vm((GROUP - 1, SLICE, 128), BF16), vm((SLICE, 128), F32), vm((SLICE, 128), BF16),
        vm((Z - 1, 16, 128), BF16), vm((SLICE, 128), BF16), vm((16, 512), BF16), pltpu.SMEM((1, 1), F32),
        dma((9,)), dma((8, 2)), dma((8, 2)), dma((8, 2)), dma((8, 2)),
        dma((8, 2, 2)), dma((8, 2, 2)),
        dma((3,)), dma((3,)), dma((7,)), dma((7,)), dma((2,)), dma((2,)), dma((7,)), dma((7,)),
        dma((7,)), dma((7,)), dma((3,)), dma((3,)),
        dma((3,)), dma((3,)), dma((15,)), dma((15,)), dma((2, GROUP - 1)), dma((2, GROUP - 1)),
        dma((TILES,)), dma((Z - 1,)), dma((Z - 1,)), dma((TILES,)), dma((2, GROUP - 1)), dma((2, GROUP - 1)),
    ]
    loss, grad_first, grad_second = pl.pallas_call(
        kernel,
        out_shape=(
            jax.ShapeDtypeStruct((1, 1), F32),
            jax.ShapeDtypeStruct((768, 128), BF16),
            jax.ShapeDtypeStruct((128, 512), BF16),
        ),
        in_specs=[hbm] * 6,
        out_specs=(hbm, hbm, hbm),
        scratch_shapes=scratch,
        compiler_params=pltpu.CompilerParams(
            collective_id=0, has_side_effects=True, vmem_limit_bytes=32 * 1024 * 1024
        ),
    )(*(pltpu.with_memory_space_constraint(a, pltpu.HBM) for a in (clip_feats, teacher_audio, teacher_text, w_first, w_second, pairing.reshape(1, 128))))
    grad_second, grad_first = lax.optimization_barrier((grad_second.astype(F32), grad_first))
    return loss.reshape(()), grad_first.astype(F32), grad_second


def solution(mesh):
    finer = Mesh(mesh.devices.reshape(Y, Z, XL, MP), ("y", "z", "xl", "mp"))
    return jax.shard_map(
        body,
        mesh=finer,
        in_specs=(
            P(WIDE, None),
            P(WIDE, None),
            P(WIDE + ("mp",), None),
            P(None, "mp"),
            P("mp", None),
            P(WIDE),
        ),
        out_specs=(P(), P(None, "mp"), P("mp", None)),
        check_vma=False,
    )
```
